32 devices in a mesh: rep: 2 (over x), shard: 16 (over z, y, core).
Axes of the slice: x: 2, y: 2, z: 4, core: 2. Of those that a mesh axis runs over, the one named last changes fastest.
Arguments:
- hidden: bfloat16 [8192, 48], P(('rep', 'shard')), may hold values from -6 to 6
- cotangent: bfloat16 [8192, 5120], P(('rep', 'shard')), may hold values from -6 to 6
- master: float32 [48, 5120], P('shard'), may hold values from -0.078125 to 0.078125
- moment: float32 [48, 5120], P('shard'), may hold values from -6 to 6
- second: float32 [48, 5120], P('shard'), may hold values from 0.1 to 10
Outputs:
- input_grad: bfloat16 [8192, 48], P(('rep', 'shard'))
- master_new: float32 [48, 5120], P('shard')
- moment_new: float32 [48, 5120], P('shard')
- second_new: float32 [48, 5120], P('shard')
- updated_weights: bfloat16 [48, 5120], replicated
The draws below stay inside these ranges and needn't reach their ends.
All inputs are finite; a program needn't handle non-finite values.
Results may differ from the reference program's by a relative error of at most 0.0059.
Values may be sent and summed in bfloat16 or wider, within the bound.
No kernel may reach another device: no remote copies, remote signals or barrier semaphores. Data moves between devices by JAX's collectives and lax.ppermute only.
A program may use at most 64 MiB of HBM per device.

```python
import math
import jax
import jax.numpy as jnp

D = 5120
ROWS = 48
TOKENS = 8192


def spiked(drawn, stream_key, source, target, blocks, factor):
    def block_of(axis_at):
        return (jnp.arange(drawn.shape[axis_at]) // (drawn.shape[axis_at] // blocks)).reshape((-1,) + (1,) * (drawn.ndim - 1 - axis_at))

    one_side = jax.random.permutation(stream_key, blocks)[block_of(target)]
    far = (block_of(target) + blocks // 2) % blocks
    return jnp.where((block_of(source) == one_side) | (block_of(source) == far), factor * drawn, drawn)


def block_levels(own_key, dims, shards, least, largest):
    gain = 1.0
    for axis_at, shards_of in shards:
        heights = jax.random.uniform(jax.random.fold_in(jax.random.fold_in(own_key, 6), axis_at), (shards_of,), jnp.float32, least / len(shards), largest / len(shards))
        gain = gain * jnp.repeat(jnp.exp(heights), dims[axis_at] // shards_of).reshape((-1,) + (1,) * (len(dims) - 1 - axis_at))
    return gain


def gaussian(stream_key, dims, width, bound, split=(), held_as=jnp.bfloat16):
    level = block_levels(stream_key, dims, split, -0.22, 0.18) if split else 1.0
    drawn = jax.random.normal(stream_key, dims, jnp.float32) * width * level
    return jnp.minimum(jnp.maximum(drawn, -bound), bound).astype(held_as)


def gaussian_with(key, dims, scale, limit, split, heavy, dtype=jnp.bfloat16):
    values = scale * jax.random.normal(key, dims, jnp.float32)
    if split:
        values = values * block_levels(key, dims, split, -0.22, 0.18)
    return jnp.clip(spiked(values, jax.random.fold_in(key, 3), *heavy), -limit, limit).astype(dtype)


def setup_inputs(seed: int = 0) -> dict:
    seeds = jax.random.split(jax.random.key(seed), 6)
    hidden = gaussian_with(seeds[0], (TOKENS, ROWS), 1.0, 6.0, ((0, 32),), (0, 1, 16, 2.0))
    cotangent = gaussian(seeds[1], (TOKENS, D), 1.0, 6.0, ((0, 32),))
    master = gaussian(seeds[2], (ROWS, D), D ** -0.5, 0.078125, ((0, 16),), jnp.float32)
    moment = gaussian(seeds[3], (ROWS, D), 1.0, 6.0, ((0, 16),), jnp.float32)
    second = jnp.clip(jnp.exp(math.log(10.0) - 4.6051702 * jax.random.uniform(seeds[4], (ROWS, D), jnp.float32) ** block_levels(seeds[4], (ROWS, D), ((0, 16),), -0.2, 0.2)), 0.1, 10.0)
    return {"hidden": hidden, "cotangent": cotangent, "master": master, "moment": moment, "second": second}


def adam_update(master, moment, second, gradient):
    moment_new = 0.9 * moment + 0.1 * gradient
    second_new = 0.95 * second + 0.05 * gradient * gradient
    first_fix = moment_new / (1.0 - 0.9 ** 10)
    second_fix = second_new / (1.0 - 0.95 ** 10)
    master_new = master - 0.01 * (first_fix / (jnp.sqrt(second_fix) + 1e-08) + 0.1 * master)
    return (master_new, moment_new, second_new)

def reference(hidden, cotangent, master, moment, second):
    weights = master.astype(jnp.bfloat16)
    input_grad = jnp.dot(cotangent, weights.T, preferred_element_type=jnp.float32).astype(jnp.bfloat16)
    gradient = jnp.dot(hidden.T, cotangent, preferred_element_type=jnp.float32) * (1.0 / jnp.sqrt(jnp.float32(TOKENS)))
    master_new, moment_new, second_new = adam_update(master, moment, second, gradient)
    return (input_grad, master_new, moment_new, second_new, master_new.astype(jnp.bfloat16))
```

```python
import functools
import math

import jax
import jax.numpy as jnp
from jax import lax
from jax.experimental import pallas as pl
from jax.experimental.pallas import tpu as pltpu
from jax.sharding import Mesh, PartitionSpec as P

F32 = jnp.float32
BF16 = jnp.bfloat16
VMEM = pl.BlockSpec(memory_space=pltpu.VMEM)
CORES = 2
LOW = 2
COT_COPIES = 4
OUT_COPIES = 5
MAIN = 3 * 10**9
CHIPS = ("rep", "high", "low")


def call(body, outs, name, ins, cost=1_000_000, **more):
    more = {"in_specs": [VMEM] * len(ins), "out_specs": (VMEM,) * len(outs), **more}
    return pl.pallas_call(
        body,
        out_shape=tuple(jax.ShapeDtypeStruct(*out) for out in outs),
        name=name,
        cost_estimate=pl.CostEstimate(flops=cost, bytes_accessed=1_000_000, transcendentals=0),
        compiler_params=pltpu.CompilerParams(vmem_limit_bytes=16 * 2**20),
        **more,
    )(*ins)


def parity(bits, chips):
    total = 0
    for i in range(chips.bit_length() - 1):
        total = total ^ ((bits >> i) & 1)
    return total


def swap(value, rep, chip, core=0):
    chips = lax.axis_size("high") * LOW
    bits = (rep * chips + chip) * CORES + (core ^ parity(chip, chips))
    count = lax.axis_size("rep") * chips * CORES
    return lax.ppermute(value, (*CHIPS, "core"), [(i, i ^ bits) for i in range(count)])


def one_hot(rows, per, high):
    at = lax.broadcasted_iota(jnp.int32, (rows, rows), 0)
    block = jnp.floor((at.astype(F32) + 0.5) * (1.0 / per)).astype(jnp.int32)
    chips = high * LOW
    low, here = lax.axis_index("low"), lax.axis_index("high")
    last = high.bit_length() - 2
    far = (block & 1) << last
    for i in range(last):
        far = far | ((((block >> (last - i)) & 1) ^ ((here >> i) & 1)) << i)
    chip = far * LOW + (low ^ ((block & (chips - 1)) // high))
    other = parity(chip ^ (here * LOW + low), chips)
    core = lax.axis_index("core") ^ (block // chips) ^ other
    source = (chip * CORES + core) * per + at - block * per
    return (lax.broadcasted_iota(jnp.int32, (rows, rows), 1) == source).astype(BF16)


def dot(a, b, ca, cb):
    return lax.dot_general(a, b, (((ca,), (cb,)), ((), ())), preferred_element_type=F32)


def columns(dx, width):
    return pl.ds(pl.multiple_of((lax.axis_index("rep") ^ dx) * width, 128), width)


def folds(rows, width):
    some = [f for f in range(1, 9) if width % (128 * f) == 0]
    return min(some, key=lambda f: (-(-rows * f // 8) * 8 * (width // f), f))


def folded(rows, width):
    f = folds(rows, width)
    return (rows * f, width // f)


def fold(value):
    f = folds(*value.shape)
    width = value.shape[1] // f
    return jnp.concatenate([value[:, i * width : (i + 1) * width] for i in range(f)], axis=0)


def unfold(value, rows):
    f = value.shape[0] // rows
    return jnp.concatenate([value[i * rows : (i + 1) * rows] for i in range(f)], axis=1)


def partial_body(per, high, hid_hbm, cot_hbm, keep_ref, send_ref, cot_ref, hid, sems):
    rows, width = hid.shape[0], cot_ref.shape[1]
    tile = width // COT_COPIES
    pieces = [(hid_hbm, hid)]
    pieces += [
        (cot_hbm.at[:, pl.ds(i * tile, tile)], cot_ref.at[:, pl.ds(i * tile, tile)])
        for i in range(COT_COPIES)
    ]
    copies = [pltpu.make_async_copy(a, b, sems.at[i]) for i, (a, b) in enumerate(pieces)]
    for copy in copies:
        copy.start()
    move = one_hot(rows, per, high)
    copies[0].wait()
    moved = dot(move, hid[...], 1, 0).astype(BF16)
    for i in range(COT_COPIES):
        copies[1 + i].wait()
        cols = pl.ds(i * tile, tile)
        g = dot(moved, cot_ref[:, cols], 1, 0)
        keep_ref[:, cols] = g[: rows // 2]
        send_ref[:, cols] = g[rows // 2 :].astype(BF16)


def middle_body(reps, near, keep_ref, recv_ref, master, moment, second, *outs):
    *outs, state_ref = outs
    width = keep_ref.shape[1] // reps
    rows = keep_ref.shape[0] // LOW
    for dx in range(reps):
        cols = columns(dx, width)
        total = keep_ref[:, cols] + recv_ref[:, cols].astype(F32)
        for low in range(LOW):
            piece = total[low * rows : (low + 1) * rows]
            out = outs[near.index((dx, low))]
            out[...] = (fold(piece) if dx or low else piece).astype(out.dtype)
    lines = [ref[:, columns(0, width)] for ref in (master, moment, second)]
    weights = lines[0].astype(BF16).astype(F32)
    lines[:1] = [weights, lines[0] - weights]
    lines += [master[:, columns(dx, width)] for dx in range(1, reps)]
    state_ref[...] = fold(jnp.concatenate(lines, axis=0)).astype(BF16)


def join(refs, rows):
    return jnp.concatenate([unfold(ref[...].astype(F32), rows) for ref in refs], axis=0)


def join_body(rows, mine, other, *refs):
    out = refs[-1]
    both = join([mine, other], rows)
    out[...] = (both if out.shape == both.shape else fold(both)).astype(BF16)


def add(refs):
    return sum(ref[...].astype(F32) for ref in refs)


def plane_body(count, *refs):
    ins, (keep, send) = refs[:count], refs[-2:]
    total = ins[0][...]
    for ref in ins[1:]:
        total = total + unfold(ref[...].astype(F32), total.shape[0])
    half = total.shape[0] // 2
    keep[...] = total[:half]
    send[...] = fold(total[half:]).astype(BF16)


def halve_body(mine, other, *outs):
    total = mine[...] + unfold(other[...].astype(F32), mine.shape[0])
    if len(outs) == 1:
        outs[0][...] = fold(total).astype(BF16)
    else:
        half = total.shape[0] // 2
        outs[0][...] = total[:half]
        outs[1][...] = fold(total[half:]).astype(BF16)


def is_second():
    return lax.axis_index("high") >= lax.axis_size("high") // 2


def arrange_body(reps, per, state, state_other, *refs):
    out, old = refs[-2:]
    mine, other = (unfold(ref[...].astype(F32), (reps + 3) * per) for ref in (state, state_other))
    first, second = jnp.where(is_second(), other, mine), jnp.where(is_second(), mine, other)
    lines = [
        jnp.concatenate([block[i * per : (i + 1) * per] for block in (first, second)], axis=0)
        for i in range(reps + 3)
    ]
    out[0] = lines[0] + lines[1]
    out[1] = lines[2]
    out[2] = lines[3]
    here, parts = lax.axis_index("rep"), [lines[0], *lines[4:]]
    rows = []
    for rep in range(reps):
        piece = parts[rep]
        for at in range(1, reps):
            piece = jnp.where(here == at, parts[rep ^ at], piece)
        rows.append(piece)
    old[...] = fold(jnp.concatenate(rows, axis=1)).astype(BF16)


def adam_update(master, moment, second, gradient):
    moment_new = 0.9 * moment + 0.1 * gradient
    second_new = 0.95 * second + 0.05 * gradient * gradient
    first_fix = moment_new / (1.0 - 0.9**10)
    second_fix = second_new / (1.0 - 0.95**10)
    master_new = master - 0.01 * (first_fix / (jnp.sqrt(second_fix) + 1e-08) + 0.1 * master)
    return (master_new, moment_new, second_new)


def own_body(factor, per, mine, other, state, grad_ref, new_ref):
    g = unfold(add([mine, other]), 2 * per) * factor
    g = g.astype(BF16).astype(F32)
    new_ref[...] = fold(adam_update(state[0], state[1], state[2], g)[0]).astype(BF16)
    grad_ref[...] = jnp.where(is_second(), g[per:], g[:per])


def copies_body(rows, mine, other, grad, small, large):
    new = join([mine, other], rows)
    small[...] = fold(new).astype(BF16)
    large[...] = fold(jnp.concatenate([new, grad[...]], axis=0)).astype(BF16)


def across_body(reps, near, per, *refs):
    _, *ins, grad, new, grad_out = refs
    width = new.shape[1] // reps
    rows = new.shape[0] // LOW
    for dx in range(reps):
        cols = columns(dx, width)
        held = [
            unfold(ins[near.index((dx, low))][...].astype(F32), rows + (per if dx and not low else 0))
            for low in range(LOW)
        ]
        new[:, cols] = jnp.concatenate([h[:rows] for h in held], axis=0).astype(BF16)
        grad_out[:, cols] = held[0][rows:] if dx else grad[...]


def product_body(old, old_other, cot, out):
    both = jnp.concatenate([old[...], old_other[...]], axis=0)
    out[...] = dot(both, cot[...], 1, 1)


def last_body(per, high, new, new_other, product, gradient, master, moment, second, *refs):
    outs, (out, grad, *states), sems = refs[:5], refs[5:10], refs[10]
    for ref, value in zip(states, adam_update(master[...], moment[...], second[...], gradient[...])):
        ref[...] = value
    move = one_hot(out.shape[0], per, high)
    grad[...] = dot(move, product[...].astype(BF16), 0, 0).astype(BF16)
    copies = [pltpu.make_async_copy(a, b, sems.at[i]) for i, (a, b) in enumerate(zip((grad, *states), outs[1:]))]
    for copy in copies:
        copy.start()
    tile = out.shape[1] // OUT_COPIES
    half = new.shape[0]
    for i in range(OUT_COPIES):
        cols = pl.ds(i * tile, tile)
        chunk = dot(move[:half], new[:, cols], 0, 0) + dot(move[half:], new_other[:, cols], 0, 0)
        out[:, cols] = chunk.astype(BF16)
        copies.append(pltpu.make_async_copy(out.at[:, cols], outs[0].at[:, cols], sems.at[4 + i]))
        copies[-1].start()
    for copy in copies:
        copy.wait()


def local(hidden, cotangent, master, moment, second):
    reps, high = lax.axis_size("rep"), lax.axis_size("high")
    shards = high * LOW * CORES
    per, width = master.shape
    rows, part, tokens = shards * per, width // reps, hidden.shape[0]
    block = high * per
    factor = 1.0 / math.sqrt(tokens * reps * shards)
    far = [1 << i for i in range(high.bit_length() - 1)]
    halved, last = far[:-1], far[-1]
    near = sorted(((dx, low) for dx in range(reps) for low in range(LOW)),
                  key=lambda c: (c != (0, 0), -bool(c[0]) - bool(c[1]), c))
    states = (master, moment, second)

    ins = [pltpu.with_memory_space_constraint(x, pltpu.HBM) for x in (hidden.T, cotangent)]
    keep, send, cot = call(
        functools.partial(partial_body, per, high),
        [((rows // 2, width), F32), ((rows // 2, width), BF16), (cotangent.shape, BF16)],
        "partial", ins,
        cost=2 * rows * width * tokens,
        in_specs=[pl.BlockSpec(memory_space=pltpu.HBM)] * 2,
        scratch_shapes=[pltpu.VMEM((rows, tokens), BF16), pltpu.SemaphoreType.DMA((COT_COPIES + 1,))],
    )

    recv = swap(send, 0, 0, 1)
    *pieces, state = call(
        functools.partial(middle_body, reps, near),
        [*((folded(block, part), BF16) if i else ((block, part), F32) for i in range(len(near))),
         (folded((reps + 3) * per, part), BF16)],
        "middle", [keep, recv, *states],
    )
    pieces = [pieces[0]] + [swap(p, dx, low) for p, (dx, low) in zip(pieces[1:], near[1:])]
    state_other = swap(state, 0, last * LOW)
    lines = block // 2
    body = functools.partial(plane_body, len(near))
    for bits in halved:
        keep, send = call(body, [((lines, part), F32), (folded(lines, part), BF16)], "halve", pieces)
        pieces, body, lines = [keep, swap(send, 0, bits * LOW)], halve_body, lines // 2
    (total,) = call(halve_body, [(folded(2 * per, part), BF16)], "whole", pieces)
    other = swap(total, 0, last * LOW)
    state, old = call(
        functools.partial(arrange_body, reps, per),
        [((3, 2 * per, part), F32), (folded(2 * per, width), BF16)],
        "arrange", [state, state_other, total],
    )
    grad, new = call(
        functools.partial(own_body, factor, per), [((per, part), F32), (folded(2 * per, part), BF16)],
        "own", [total, other, state], cost=MAIN,
    )

    lines = 2 * per
    for bits in reversed(halved):
        new_other = swap(new, 0, bits * LOW)
        if bits == halved[0]:
            small, large = call(
                functools.partial(copies_body, lines),
                [(folded(2 * lines, part), BF16), (folded(2 * lines + per, part), BF16)],
                "copies", [new, new_other, grad], cost=MAIN,
            )
        else:
            (new,) = call(functools.partial(join_body, lines), [(folded(2 * lines, part), BF16)],
                          "join", [new, new_other])
        lines *= 2
    lines = 2 * per
    for chip in [bits * LOW for bits in reversed(halved)] + [1]:
        old_other = swap(old, 0, chip)
        shape = (2 * lines, width) if chip == 1 else folded(2 * lines, width)
        (old,) = call(functools.partial(join_body, lines), [(shape, BF16)], "join_old",
                      [old, old_other] + ([] if chip == 1 else [grad]))
        lines *= 2
    old_other = swap(old, 0, 0, 1)
    near = [near[0], *reversed(near[1:])]
    pieces = [small] + [swap(large if dx and not low else small, dx, low) for dx, low in near[1:]]
    new, grad = call(
        functools.partial(across_body, reps, near, per),
        [((rows // 2, width), BF16), ((per, width), F32)],
        "across", [old, *pieces, grad],
    )
    new_other = swap(new, 0, 0, 1)
    (product,) = call(product_body, [((rows, tokens), F32)], "product", [old, old_other, cot],
                      cost=2 * rows * width * tokens)
    outs = [((rows, width), BF16), ((rows, tokens), BF16), *[((per, width), F32)] * 3]
    updated, input_grad, *states = call(
        functools.partial(last_body, per, high), outs,
        "last", [new, new_other, product, grad, *states],
        out_specs=(pl.BlockSpec(memory_space=pltpu.HBM),) * 5,
        scratch_shapes=[*(pltpu.VMEM(*out) for out in outs), pltpu.SemaphoreType.DMA((4 + OUT_COPIES,))],
    )
    return (input_grad.T, *states, updated)


def solution(mesh):
    reps, shards = mesh.shape["rep"], mesh.shape["shard"]
    split = Mesh(mesh.devices.reshape(reps, shards // LOW // CORES, LOW, CORES), (*CHIPS, "core"))
    by_row = P(("high", "low", "core"), None)
    by_token = P((*CHIPS, "core"), None)
    return jax.shard_map(
        local,
        mesh=split,
        in_specs=(by_token, by_token, by_row, by_row, by_row),
        out_specs=(by_token, by_row, by_row, by_row, P()),
        check_vma=False,
    )
```

```python
import functools
import math

import jax
import jax.numpy as jnp
from jax import lax
from jax.experimental import pallas as pl
from jax.experimental.pallas import tpu as pltpu
from jax.sharding import Mesh, PartitionSpec as P

F32 = jnp.float32
BF16 = jnp.bfloat16
VMEM = pl.BlockSpec(memory_space=pltpu.VMEM)
CORES = 2
LOW = 2
COT_COPIES = 2
OUT_COPIES = 5
MAIN = 3 * 10**9
CHIPS = ("rep", "high", "low")


def call(body, outs, name, ins, cost=1_000_000, **more):
    more = {"in_specs": [VMEM] * len(ins), "out_specs": (VMEM,) * len(outs), **more}
    return pl.pallas_call(
        body,
        out_shape=tuple(jax.ShapeDtypeStruct(*out) for out in outs),
        name=name,
        cost_estimate=pl.CostEstimate(flops=cost, bytes_accessed=1_000_000, transcendentals=0),
        compiler_params=pltpu.CompilerParams(vmem_limit_bytes=16 * 2**20),
        **more,
    )(*ins)


def parity(bits, chips):
    total = 0
    for i in range(chips.bit_length() - 1):
        total = total ^ ((bits >> i) & 1)
    return total


def swap(value, rep, chip, core=0):
    chips = lax.axis_size("high") * LOW
    bits = (rep * chips + chip) * CORES + (core ^ parity(chip, chips))
    count = lax.axis_size("rep") * chips * CORES
    return lax.ppermute(value, (*CHIPS, "core"), [(i, i ^ bits) for i in range(count)])


def one_hot(rows, per, high):
    at = lax.broadcasted_iota(jnp.int32, (rows, rows), 0)
    block = jnp.floor((at.astype(F32) + 0.5) * (1.0 / per)).astype(jnp.int32)
    chips = high * LOW
    low, here = lax.axis_index("low"), lax.axis_index("high")
    last = high.bit_length() - 2
    far = (block & 1) << last
    for i in range(last):
        far = far | ((((block >> (last - i)) & 1) ^ ((here >> i) & 1)) << i)
    chip = far * LOW + (low ^ ((block & (chips - 1)) // high))
    other = parity(chip ^ (here * LOW + low), chips)
    core = lax.axis_index("core") ^ (block // chips) ^ other
    source = (chip * CORES + core) * per + at - block * per
    return (lax.broadcasted_iota(jnp.int32, (rows, rows), 1) == source).astype(BF16)


def dot(a, b, ca, cb):
    return lax.dot_general(a, b, (((ca,), (cb,)), ((), ())), preferred_element_type=F32)


def columns(dx, width):
    return pl.ds(pl.multiple_of((lax.axis_index("rep") ^ dx) * width, 128), width)


def folds(rows, width):
    some = [f for f in range(1, 9) if width % (128 * f) == 0]
    return min(some, key=lambda f: (-(-rows * f // 8) * 8 * (width // f), f))


def folded(rows, width):
    f = folds(rows, width)
    return (rows * f, width // f)


def fold(value):
    f = folds(*value.shape)
    width = value.shape[1] // f
    return jnp.concatenate([value[:, i * width : (i + 1) * width] for i in range(f)], axis=0)


def unfold(value, rows):
    f = value.shape[0] // rows
    return jnp.concatenate([value[i * rows : (i + 1) * rows] for i in range(f)], axis=1)


def partial_body(per, high, hid_hbm, cot_hbm, keep_ref, send_ref, cot_ref, hid, sems):
    rows, width = hid.shape[0], cot_ref.shape[1]
    tile = width // COT_COPIES
    pieces = [(hid_hbm, hid)]
    pieces += [
        (cot_hbm.at[:, pl.ds(i * tile, tile)], cot_ref.at[:, pl.ds(i * tile, tile)])
        for i in range(COT_COPIES)
    ]
    copies = [pltpu.make_async_copy(a, b, sems.at[i]) for i, (a, b) in enumerate(pieces)]
    for copy in copies:
        copy.start()
    move = one_hot(rows, per, high)
    copies[0].wait()
    moved = dot(move, hid[...], 1, 0).astype(BF16)
    for i in range(COT_COPIES):
        copies[1 + i].wait()
        cols = pl.ds(i * tile, tile)
        g = dot(moved, cot_ref[:, cols], 1, 0)
        keep_ref[:, cols] = g[: rows // 2]
        send_ref[:, cols] = g[rows // 2 :].astype(BF16)


def middle_body(reps, near, keep_ref, recv_ref, master, moment, second, *outs):
    *outs, state_ref = outs
    width = keep_ref.shape[1] // reps
    rows = keep_ref.shape[0] // LOW
    for dx in range(reps):
        cols = columns(dx, width)
        total = keep_ref[:, cols] + recv_ref[:, cols].astype(F32)
        for low in range(LOW):
            piece = total[low * rows : (low + 1) * rows]
            out = outs[near.index((dx, low))]
            out[...] = (fold(piece) if dx or low else piece).astype(out.dtype)
    lines = [ref[:, columns(0, width)] for ref in (master, moment, second)]
    weights = lines[0].astype(BF16).astype(F32)
    lines[:1] = [weights, lines[0] - weights]
    lines += [master[:, columns(dx, width)] for dx in range(1, reps)]
    state_ref[...] = fold(jnp.concatenate(lines, axis=0)).astype(BF16)


def join(refs, rows):
    return jnp.concatenate([unfold(ref[...].astype(F32), rows) for ref in refs], axis=0)


def join_body(rows, mine, other, *refs):
    out = refs[-1]
    both = join([mine, other], rows)
    out[...] = (both if out.shape == both.shape else fold(both)).astype(BF16)


def add(refs):
    return sum(ref[...].astype(F32) for ref in refs)


def plane_body(count, *refs):
    ins, (keep, send) = refs[:count], refs[-2:]
    total = ins[0][...]
    for ref in ins[1:]:
        total = total + unfold(ref[...].astype(F32), total.shape[0])
    half = total.shape[0] // 2
    keep[...] = total[:half]
    send[...] = fold(total[half:]).astype(BF16)


def halve_body(mine, other, *outs):
    total = mine[...] + unfold(other[...].astype(F32), mine.shape[0])
    if len(outs) == 1:
        outs[0][...] = fold(total).astype(BF16)
    else:
        half = total.shape[0] // 2
        outs[0][...] = total[:half]
        outs[1][...] = fold(total[half:]).astype(BF16)


def is_second():
    return lax.axis_index("high") >= lax.axis_size("high") // 2


def arrange_body(reps, per, state, state_other, *refs):
    out, old = refs[-2:]
    mine, other = (unfold(ref[...].astype(F32), (reps + 3) * per) for ref in (state, state_other))
    first, second = jnp.where(is_second(), other, mine), jnp.where(is_second(), mine, other)
    lines = [
        jnp.concatenate([block[i * per : (i + 1) * per] for block in (first, second)], axis=0)
        for i in range(reps + 3)
    ]
    out[0] = lines[0] + lines[1]
    out[1] = lines[2]
    out[2] = lines[3]
    here, parts = lax.axis_index("rep"), [lines[0], *lines[4:]]
    rows = []
    for rep in range(reps):
        piece = parts[rep]
        for at in range(1, reps):
            piece = jnp.where(here == at, parts[rep ^ at], piece)
        rows.append(piece)
    old[...] = fold(jnp.concatenate(rows, axis=1)).astype(BF16)


def adam_update(master, moment, second, gradient):
    moment_new = 0.9 * moment + 0.1 * gradient
    second_new = 0.95 * second + 0.05 * gradient * gradient
    first_fix = moment_new / (1.0 - 0.9**10)
    second_fix = second_new / (1.0 - 0.95**10)
    master_new = master - 0.01 * (first_fix / (jnp.sqrt(second_fix) + 1e-08) + 0.1 * master)
    return (master_new, moment_new, second_new)


def own_body(factor, per, mine, other, state, grad_ref, new_ref):
    g = unfold(add([mine, other]), 2 * per) * factor
    g = g.astype(BF16).astype(F32)
    new_ref[...] = fold(adam_update(state[0], state[1], state[2], g)[0]).astype(BF16)
    grad_ref[...] = jnp.where(is_second(), g[per:], g[:per]).astype(BF16)


def across_body(reps, near, *refs):
    *ins, new = refs[-len(near) - 1 :]
    width = new.shape[1] // reps
    for dx in range(reps):
        pieces = [ins[near.index((dx, low))] for low in range(LOW)]
        new[:, columns(dx, width)] = join(pieces, new.shape[0] // LOW).astype(BF16)


def wide_body(*refs):
    *ins, out = refs
    for dx, ref in enumerate(ins):
        out[:, columns(dx, ref.shape[1])] = ref[...].astype(F32)


def product_body(old, old_other, cot, out):
    both = jnp.concatenate([old[...], old_other[...]], axis=0)
    out[...] = dot(both, cot[...], 1, 1)


def last_body(per, high, new, new_other, product, gradient, master, moment, second, *refs):
    outs, (out, grad, *states), sems = refs[:5], refs[5:10], refs[10]
    for ref, value in zip(states, adam_update(master[...], moment[...], second[...], gradient[...])):
        ref[...] = value
    move = one_hot(out.shape[0], per, high)
    grad[...] = dot(move, product[...].astype(BF16), 0, 0).astype(BF16)
    copies = [pltpu.make_async_copy(a, b, sems.at[i]) for i, (a, b) in enumerate(zip((grad, *states), outs[1:]))]
    for copy in copies:
        copy.start()
    tile = out.shape[1] // OUT_COPIES
    half = new.shape[0]
    for i in range(OUT_COPIES):
        cols = pl.ds(i * tile, tile)
        chunk = dot(move[:half], new[:, cols], 0, 0) + dot(move[half:], new_other[:, cols], 0, 0)
        out[:, cols] = chunk.astype(BF16)
        copies.append(pltpu.make_async_copy(out.at[:, cols], outs[0].at[:, cols], sems.at[4 + i]))
        copies[-1].start()
    for copy in copies:
        copy.wait()


def local(hidden, cotangent, master, moment, second):
    reps, high = lax.axis_size("rep"), lax.axis_size("high")
    shards = high * LOW * CORES
    per, width = master.shape
    rows, part, tokens = shards * per, width // reps, hidden.shape[0]
    block = high * per
    factor = 1.0 / math.sqrt(tokens * reps * shards)
    far = [1 << i for i in range(high.bit_length() - 1)]
    halved, last = far[:-1], far[-1]
    near = sorted(((dx, low) for dx in range(reps) for low in range(LOW)),
                  key=lambda c: (c != (0, 0), -bool(c[0]) - bool(c[1]), c))
    states = (master, moment, second)

    ins = [pltpu.with_memory_space_constraint(x, pltpu.HBM) for x in (hidden.T, cotangent)]
    keep, send, cot = call(
        functools.partial(partial_body, per, high),
        [((rows // 2, width), F32), ((rows // 2, width), BF16), (cotangent.shape, BF16)],
        "partial", ins,
        cost=2 * rows * width * tokens,
        in_specs=[pl.BlockSpec(memory_space=pltpu.HBM)] * 2,
        scratch_shapes=[pltpu.VMEM((rows, tokens), BF16), pltpu.SemaphoreType.DMA((COT_COPIES + 1,))],
    )

    recv = swap(send, 0, 0, 1)
    *pieces, state = call(
        functools.partial(middle_body, reps, near),
        [*((folded(block, part), BF16) if i else ((block, part), F32) for i in range(len(near))),
         (folded((reps + 3) * per, part), BF16)],
        "middle", [keep, recv, *states],
    )
    pieces = [pieces[0]] + [swap(p, dx, low) for p, (dx, low) in zip(pieces[1:], near[1:])]
    state_other = swap(state, 0, last * LOW)
    lines = block // 2
    body = functools.partial(plane_body, len(near))
    for bits in halved:
        keep, send = call(body, [((lines, part), F32), (folded(lines, part), BF16)], "halve", pieces)
        pieces, body, lines = [keep, swap(send, 0, bits * LOW)], halve_body, lines // 2
    (total,) = call(halve_body, [(folded(2 * per, part), BF16)], "whole", pieces)
    other = swap(total, 0, last * LOW)
    state, old = call(
        functools.partial(arrange_body, reps, per),
        [((3, 2 * per, part), F32), (folded(2 * per, width), BF16)],
        "arrange", [state, state_other, total],
    )
    grad, new = call(
        functools.partial(own_body, factor, per), [((per, part), BF16), (folded(2 * per, part), BF16)],
        "own", [total, other, state], cost=MAIN,
    )

    lines = 2 * per
    for bits in reversed(halved):
        body = functools.partial(join_body, lines)
        lines *= 2
        (new,) = call(body, [(folded(lines, part), BF16)], "copies", [new, swap(new, 0, bits * LOW)], cost=MAIN)
    grads = [grad] + [swap(grad, dx, 0) for dx in range(1, reps)]
    lines = 2 * per
    for chip in [bits * LOW for bits in reversed(halved)] + [1]:
        old_other = swap(old, 0, chip)
        shape = (2 * lines, width) if chip == 1 else folded(2 * lines, width)
        (old,) = call(functools.partial(join_body, lines), [(shape, BF16)], "join_old",
                      [old, old_other] + ([] if chip == 1 else [grad]))
        lines *= 2
    old_other = swap(old, 0, 0, 1)
    near = [near[0], *reversed(near[1:])]
    pieces = [swap(new, *c) if any(c) else new for c in near]
    (new,) = call(functools.partial(across_body, reps, near), [((rows // 2, width), BF16)],
                  "across", [old, *pieces])
    new_other = swap(new, 0, 0, 1)
    (product,) = call(product_body, [((rows, tokens), F32)], "product", [old, old_other, cot],
                      cost=2 * rows * width * tokens)
    (grad,) = call(wide_body, [((per, width), F32)], "gradient", grads, cost=MAIN)
    outs = [((rows, width), BF16), ((rows, tokens), BF16), *[((per, width), F32)] * 3]
    updated, input_grad, *states = call(
        functools.partial(last_body, per, high), outs,
        "last", [new, new_other, product, grad, *states],
        out_specs=(pl.BlockSpec(memory_space=pltpu.HBM),) * 5,
        scratch_shapes=[*(pltpu.VMEM(*out) for out in outs), pltpu.SemaphoreType.DMA((4 + OUT_COPIES,))],
    )
    return (input_grad.T, *states, updated)


def solution(mesh):
    reps, shards = mesh.shape["rep"], mesh.shape["shard"]
    split = Mesh(mesh.devices.reshape(reps, shards // LOW // CORES, LOW, CORES), (*CHIPS, "core"))
    by_row = P(("high", "low", "core"), None)
    by_token = P((*CHIPS, "core"), None)
    return jax.shard_map(
        local,
        mesh=split,
        in_specs=(by_token, by_token, by_row, by_row, by_row),
        out_specs=(by_token, by_row, by_row, by_row, P()),
        check_vma=False,
    )
```

```python
import functools
import math

import jax
import jax.numpy as jnp
from jax import lax
from jax.experimental import pallas as pl
from jax.experimental.pallas import tpu as pltpu
from jax.sharding import Mesh, PartitionSpec as P

F32 = jnp.float32
BF16 = jnp.bfloat16
VMEM = pl.BlockSpec(memory_space=pltpu.VMEM)
CORES = 2
LOW = 2
COT_COPIES = 2
OUT_COPIES = 5
MAIN = 3 * 10**9
CHIPS = ("rep", "high", "low")


def call(body, outs, name, ins, cost=1_000_000, **more):
    more = {"in_specs": [VMEM] * len(ins), "out_specs": (VMEM,) * len(outs), **more}
    return pl.pallas_call(
        body,
        out_shape=tuple(jax.ShapeDtypeStruct(*out) for out in outs),
        name=name,
        cost_estimate=pl.CostEstimate(flops=cost, bytes_accessed=1_000_000, transcendentals=0),
        compiler_params=pltpu.CompilerParams(vmem_limit_bytes=16 * 2**20),
        **more,
    )(*ins)


def parity(bits, chips):
    total = 0
    for i in range(chips.bit_length() - 1):
        total = total ^ ((bits >> i) & 1)
    return total


def swap(value, rep, chip, core=0):
    chips = lax.axis_size("high") * LOW
    bits = (rep * chips + chip) * CORES + (core ^ parity(chip, chips))
    count = lax.axis_size("rep") * chips * CORES
    return lax.ppermute(value, (*CHIPS, "core"), [(i, i ^ bits) for i in range(count)])


def one_hot(rows, per, high):
    at = lax.broadcasted_iota(jnp.int32, (rows, rows), 0)
    block = jnp.floor((at.astype(F32) + 0.5) * (1.0 / per)).astype(jnp.int32)
    chips = high * LOW
    low, here = lax.axis_index("low"), lax.axis_index("high")
    last = high.bit_length() - 2
    far = (block & 1) << last
    for i in range(last):
        far = far | ((((block >> (last - i)) & 1) ^ ((here >> i) & 1)) << i)
    chip = far * LOW + (low ^ ((block & (chips - 1)) // high))
    other = parity(chip ^ (here * LOW + low), chips)
    core = lax.axis_index("core") ^ (block // chips) ^ other
    source = (chip * CORES + core) * per + at - block * per
    return (lax.broadcasted_iota(jnp.int32, (rows, rows), 1) == source).astype(BF16)


def dot(a, b, ca, cb):
    return lax.dot_general(a, b, (((ca,), (cb,)), ((), ())), preferred_element_type=F32)


def columns(dx, width):
    return pl.ds(pl.multiple_of((lax.axis_index("rep") ^ dx) * width, 128), width)


def folds(rows, width):
    some = [f for f in range(1, 9) if width % (128 * f) == 0]
    return min(some, key=lambda f: (-(-rows * f // 8) * 8 * (width // f), f))


def folded(rows, width):
    f = folds(rows, width)
    return (rows * f, width // f)


def fold(value):
    f = folds(*value.shape)
    width = value.shape[1] // f
    return jnp.concatenate([value[:, i * width : (i + 1) * width] for i in range(f)], axis=0)


def unfold(value, rows):
    f = value.shape[0] // rows
    return jnp.concatenate([value[i * rows : (i + 1) * rows] for i in range(f)], axis=1)


def partial_body(per, high, hid_hbm, cot_hbm, keep_ref, send_ref, cot_ref, hid, sems):
    rows, width = hid.shape[0], cot_ref.shape[1]
    tile = width // COT_COPIES
    pieces = [(hid_hbm, hid)]
    pieces += [
        (cot_hbm.at[:, pl.ds(i * tile, tile)], cot_ref.at[:, pl.ds(i * tile, tile)])
        for i in range(COT_COPIES)
    ]
    copies = [pltpu.make_async_copy(a, b, sems.at[i]) for i, (a, b) in enumerate(pieces)]
    for copy in copies:
        copy.start()
    move = one_hot(rows, per, high)
    copies[0].wait()
    moved = dot(move, hid[...], 1, 0).astype(BF16)
    for i in range(COT_COPIES):
        copies[1 + i].wait()
        cols = pl.ds(i * tile, tile)
        g = dot(moved, cot_ref[:, cols], 1, 0)
        keep_ref[:, cols] = g[: rows // 2]
        send_ref[:, cols] = g[rows // 2 :].astype(BF16)


def middle_body(reps, near, keep_ref, recv_ref, master, moment, second, *outs):
    *outs, state_ref = outs
    width = keep_ref.shape[1] // reps
    rows = keep_ref.shape[0] // LOW
    for dx in range(reps):
        cols = columns(dx, width)
        total = keep_ref[:, cols] + recv_ref[:, cols].astype(F32)
        for low in range(LOW):
            piece = total[low * rows : (low + 1) * rows]
            out = outs[near.index((dx, low))]
            out[...] = (fold(piece) if dx or low else piece).astype(out.dtype)
    lines = [ref[:, columns(0, width)] for ref in (master, moment, second)]
    weights = lines[0].astype(BF16).astype(F32)
    lines[:1] = [weights, lines[0] - weights]
    lines += [master[:, columns(dx, width)] for dx in range(1, reps)]
    state_ref[...] = fold(jnp.concatenate(lines, axis=0)).astype(BF16)


def join(refs, rows):
    return jnp.concatenate([unfold(ref[...].astype(F32), rows) for ref in refs], axis=0)


def join_body(rows, mine, other, *refs):
    out = refs[-1]
    both = join([mine, other], rows)
    out[...] = (both if out.shape == both.shape else fold(both)).astype(BF16)


def add(refs):
    return sum(ref[...].astype(F32) for ref in refs)


def plane_body(count, *refs):
    ins, (keep, send) = refs[:count], refs[-2:]
    total = ins[0][...]
    for ref in ins[1:]:
        total = total + unfold(ref[...].astype(F32), total.shape[0])
    half = total.shape[0] // 2
    keep[...] = total[:half]
    send[...] = fold(total[half:]).astype(BF16)


def halve_body(mine, other, *outs):
    total = mine[...] + unfold(other[...].astype(F32), mine.shape[0])
    if len(outs) == 1:
        outs[0][...] = fold(total).astype(BF16)
    else:
        half = total.shape[0] // 2
        outs[0][...] = total[:half]
        outs[1][...] = fold(total[half:]).astype(BF16)


def is_second():
    return lax.axis_index("high") >= lax.axis_size("high") // 2


def arrange_body(reps, per, state, state_other, *refs):
    out, old = refs[-2:]
    mine, other = (unfold(ref[...].astype(F32), (reps + 3) * per) for ref in (state, state_other))
    first, second = jnp.where(is_second(), other, mine), jnp.where(is_second(), mine, other)
    lines = [
        jnp.concatenate([block[i * per : (i + 1) * per] for block in (first, second)], axis=0)
        for i in range(reps + 3)
    ]
    out[0] = lines[0] + lines[1]
    out[1] = lines[2]
    out[2] = lines[3]
    here, parts = lax.axis_index("rep"), [lines[0], *lines[4:]]
    rows = []
    for rep in range(reps):
        piece = parts[rep]
        for at in range(1, reps):
            piece = jnp.where(here == at, parts[rep ^ at], piece)
        rows.append(piece)
    old[...] = fold(jnp.concatenate(rows, axis=1)).astype(BF16)


def adam_update(master, moment, second, gradient):
    moment_new = 0.9 * moment + 0.1 * gradient
    second_new = 0.95 * second + 0.05 * gradient * gradient
    first_fix = moment_new / (1.0 - 0.9**10)
    second_fix = second_new / (1.0 - 0.95**10)
    master_new = master - 0.01 * (first_fix / (jnp.sqrt(second_fix) + 1e-08) + 0.1 * master)
    return (master_new, moment_new, second_new)


def own_body(factor, per, mine, other, state, grad_ref, new_ref):
    g = unfold(add([mine, other]), 2 * per) * factor
    g = g.astype(BF16).astype(F32)
    new_ref[...] = fold(adam_update(state[0], state[1], state[2], g)[0]).astype(BF16)
    grad_ref[...] = jnp.where(is_second(), g[per:], g[:per]).astype(BF16)


def across_body(reps, near, *refs):
    *ins, new = refs[-len(near) - 1 :]
    width = new.shape[1] // reps
    for dx in range(reps):
        pieces = [ins[near.index((dx, low))] for low in range(LOW)]
        new[:, columns(dx, width)] = join(pieces, new.shape[0] // LOW).astype(BF16)


def wide_body(*refs):
    *ins, out = refs
    for dx, ref in enumerate(ins):
        out[:, columns(dx, ref.shape[1])] = ref[...].astype(F32)


def product_body(per, high, old, old_other, cot, gradient, master, moment, second, grad, *states):
    both = jnp.concatenate([old[...], old_other[...]], axis=0)
    rows = dot(both, cot[...], 1, 1).astype(BF16)
    for ref, value in zip(states, adam_update(master[...], moment[...], second[...], gradient[...])):
        ref[...] = value
    grad[...] = dot(one_hot(grad.shape[0], per, high), rows, 0, 0).astype(BF16)


def last_body(per, high, new, new_other, *refs):
    held, outs, (out, sems) = refs[:4], refs[4:9], refs[9:]
    copies = [pltpu.make_async_copy(a, b, sems.at[i]) for i, (a, b) in enumerate(zip(held, outs[1:]))]
    for copy in copies:
        copy.start()
    move = one_hot(out.shape[0], per, high)
    tile = out.shape[1] // OUT_COPIES
    half = new.shape[0]
    for i in range(OUT_COPIES):
        cols = pl.ds(i * tile, tile)
        chunk = dot(move[:half], new[:, cols], 0, 0) + dot(move[half:], new_other[:, cols], 0, 0)
        out[:, cols] = chunk.astype(BF16)
        copies.append(pltpu.make_async_copy(out.at[:, cols], outs[0].at[:, cols], sems.at[4 + i]))
        copies[-1].start()
    for copy in copies:
        copy.wait()


def local(hidden, cotangent, master, moment, second):
    reps, high = lax.axis_size("rep"), lax.axis_size("high")
    shards = high * LOW * CORES
    per, width = master.shape
    rows, part, tokens = shards * per, width // reps, hidden.shape[0]
    block = high * per
    factor = 1.0 / math.sqrt(tokens * reps * shards)
    far = [1 << i for i in range(high.bit_length() - 1)]
    halved, last = far[:-1], far[-1]
    near = sorted(((dx, low) for dx in range(reps) for low in range(LOW)),
                  key=lambda c: (c != (0, 0), -bool(c[0]) - bool(c[1]), c))
    states = (master, moment, second)

    ins = [pltpu.with_memory_space_constraint(x, pltpu.HBM) for x in (hidden.T, cotangent)]
    keep, send, cot = call(
        functools.partial(partial_body, per, high),
        [((rows // 2, width), F32), ((rows // 2, width), BF16), (cotangent.shape, BF16)],
        "partial", ins,
        cost=2 * rows * width * tokens,
        in_specs=[pl.BlockSpec(memory_space=pltpu.HBM)] * 2,
        scratch_shapes=[pltpu.VMEM((rows, tokens), BF16), pltpu.SemaphoreType.DMA((COT_COPIES + 1,))],
    )

    recv = swap(send, 0, 0, 1)
    *pieces, state = call(
        functools.partial(middle_body, reps, near),
        [*((folded(block, part), BF16) if i else ((block, part), F32) for i in range(len(near))),
         (folded((reps + 3) * per, part), BF16)],
        "middle", [keep, recv, *states],
    )
    pieces = [pieces[0]] + [swap(p, dx, low) for p, (dx, low) in zip(pieces[1:], near[1:])]
    state_other = swap(state, 0, last * LOW)
    lines = block // 2
    body = functools.partial(plane_body, len(near))
    for bits in halved:
        keep, send = call(body, [((lines, part), F32), (folded(lines, part), BF16)], "halve", pieces)
        pieces, body, lines = [keep, swap(send, 0, bits * LOW)], halve_body, lines // 2
    (total,) = call(halve_body, [(folded(2 * per, part), BF16)], "whole", pieces)
    other = swap(total, 0, last * LOW)
    state, old = call(
        functools.partial(arrange_body, reps, per),
        [((3, 2 * per, part), F32), (folded(2 * per, width), BF16)],
        "arrange", [state, state_other, total],
    )
    grad, new = call(
        functools.partial(own_body, factor, per), [((per, part), BF16), (folded(2 * per, part), BF16)],
        "own", [total, other, state], cost=MAIN,
    )

    lines = 2 * per
    for bits in reversed(halved):
        body = functools.partial(join_body, lines)
        lines *= 2
        (new,) = call(body, [(folded(lines, part), BF16)], "copies", [new, swap(new, 0, bits * LOW)], cost=MAIN)
    grads = [grad] + [swap(grad, dx, 0) for dx in range(1, reps)]
    lines = 2 * per
    for chip in [bits * LOW for bits in reversed(halved)] + [1]:
        old_other = swap(old, 0, chip)
        shape = (2 * lines, width) if chip == 1 else folded(2 * lines, width)
        (old,) = call(functools.partial(join_body, lines), [(shape, BF16)], "join_old",
                      [old, old_other] + ([] if chip == 1 else [grad]))
        lines *= 2
    old_other = swap(old, 0, 0, 1)
    pieces = [swap(new, *c) if any(c) else new for c in near]
    (new,) = call(functools.partial(across_body, reps, near), [((rows // 2, width), BF16)],
                  "across", [old, *pieces])
    new_other = swap(new, 0, 0, 1)
    (grad,) = call(wide_body, [((per, width), F32)], "gradient", grads, cost=MAIN)
    outs = [((rows, tokens), BF16), *[((per, width), F32)] * 3]
    held = call(functools.partial(product_body, per, high), outs, "product",
                [old, old_other, cot, grad, *states], cost=2 * rows * width * tokens)
    outs = [((rows, width), BF16), *outs]
    updated, input_grad, *states = call(
        functools.partial(last_body, per, high), outs, "last", [new, new_other, *held],
        out_specs=(pl.BlockSpec(memory_space=pltpu.HBM),) * 5,
        scratch_shapes=[pltpu.VMEM(*outs[0]), pltpu.SemaphoreType.DMA((4 + OUT_COPIES,))],
    )
    return (input_grad.T, *states, updated)


def solution(mesh):
    reps, shards = mesh.shape["rep"], mesh.shape["shard"]
    split = Mesh(mesh.devices.reshape(reps, shards // LOW // CORES, LOW, CORES), (*CHIPS, "core"))
    by_row = P(("high", "low", "core"), None)
    by_token = P((*CHIPS, "core"), None)
    return jax.shard_map(
        local,
        mesh=split,
        in_specs=(by_token, by_token, by_row, by_row, by_row),
        out_specs=(by_token, by_row, by_row, by_row, P()),
        check_vma=False,
    )
```

```python
import functools
import math

import jax
import jax.numpy as jnp
from jax import lax
from jax.experimental import pallas as pl
from jax.experimental.pallas import tpu as pltpu
from jax.sharding import Mesh, PartitionSpec as P

F32 = jnp.float32
BF16 = jnp.bfloat16
VMEM = pl.BlockSpec(memory_space=pltpu.VMEM)
CORES = 2
LOW = 2
COT_COPIES = 2
ROW_COPIES = 4
OUT_COPIES = 5
MAIN = 3 * 10**9
CHIPS = ("rep", "high", "low")


def call(body, outs, name, ins, cost=1_000_000, **more):
    more = {"in_specs": [VMEM] * len(ins), "out_specs": (VMEM,) * len(outs), **more}
    return pl.pallas_call(
        body,
        out_shape=tuple(jax.ShapeDtypeStruct(*out) for out in outs),
        name=name,
        cost_estimate=pl.CostEstimate(flops=cost, bytes_accessed=1_000_000, transcendentals=0),
        compiler_params=pltpu.CompilerParams(vmem_limit_bytes=16 * 2**20),
        **more,
    )(*ins)


def parity(bits, chips):
    total = 0
    for i in range(chips.bit_length() - 1):
        total = total ^ ((bits >> i) & 1)
    return total


def swap(value, rep, chip, core=0):
    chips = lax.axis_size("high") * LOW
    bits = (rep * chips + chip) * CORES + (core ^ parity(chip, chips))
    count = lax.axis_size("rep") * chips * CORES
    return lax.ppermute(value, (*CHIPS, "core"), [(i, i ^ bits) for i in range(count)])


def one_hot(rows, per, high):
    at = lax.broadcasted_iota(jnp.int32, (rows, rows), 0)
    block = jnp.floor((at.astype(F32) + 0.5) * (1.0 / per)).astype(jnp.int32)
    chips = high * LOW
    low, here = lax.axis_index("low"), lax.axis_index("high")
    last = high.bit_length() - 2
    far = (block & 1) << last
    for i in range(last):
        far = far | ((((block >> (last - i)) & 1) ^ ((here >> i) & 1)) << i)
    chip = far * LOW + (low ^ ((block & (chips - 1)) // high))
    other = parity(chip ^ (here * LOW + low), chips)
    core = lax.axis_index("core") ^ (block // chips) ^ other
    source = (chip * CORES + core) * per + at - block * per
    return (lax.broadcasted_iota(jnp.int32, (rows, rows), 1) == source).astype(BF16)


def dot(a, b, ca, cb):
    return lax.dot_general(a, b, (((ca,), (cb,)), ((), ())), preferred_element_type=F32)


def columns(dx, width):
    return pl.ds(pl.multiple_of((lax.axis_index("rep") ^ dx) * width, 128), width)


def folds(rows, width):
    some = [f for f in range(1, 9) if width % (128 * f) == 0]
    return min(some, key=lambda f: (-(-rows * f // 8) * 8 * (width // f), f))


def folded(rows, width):
    f = folds(rows, width)
    return (rows * f, width // f)


def fold(value):
    f = folds(*value.shape)
    width = value.shape[1] // f
    return jnp.concatenate([value[:, i * width : (i + 1) * width] for i in range(f)], axis=0)


def unfold(value, rows):
    f = value.shape[0] // rows
    return jnp.concatenate([value[i * rows : (i + 1) * rows] for i in range(f)], axis=1)


def partial_body(per, high, hid_hbm, cot_hbm, keep_ref, send_ref, cot_ref, hid, sems):
    rows, width = hid.shape[0], cot_ref.shape[1]
    tile, lines = width // COT_COPIES, cot_ref.shape[0] // ROW_COPIES
    pieces = [(hid_hbm, hid)]
    for i in range(COT_COPIES):
        for j in range(ROW_COPIES):
            part = (pl.ds(j * lines, lines), pl.ds(i * tile, tile))
            pieces.append((cot_hbm.at[part], cot_ref.at[part]))
    copies = [pltpu.make_async_copy(a, b, sems.at[i]) for i, (a, b) in enumerate(pieces)]
    for copy in copies:
        copy.start()
    move = one_hot(rows, per, high)
    copies[0].wait()
    moved = dot(move, hid[...], 1, 0).astype(BF16)
    for i in range(COT_COPIES):
        for copy in copies[1 + i * ROW_COPIES : 1 + (i + 1) * ROW_COPIES]:
            copy.wait()
        cols = pl.ds(i * tile, tile)
        g = dot(moved, cot_ref[:, cols], 1, 0)
        keep_ref[:, cols] = g[: rows // 2]
        send_ref[:, cols] = g[rows // 2 :].astype(BF16)


def middle_body(reps, near, keep_ref, recv_ref, master, moment, second, *outs):
    *outs, state_ref = outs
    width = keep_ref.shape[1] // reps
    rows = keep_ref.shape[0] // LOW
    for dx in range(reps):
        cols = columns(dx, width)
        total = keep_ref[:, cols] + recv_ref[:, cols].astype(F32)
        for low in range(LOW):
            piece = total[low * rows : (low + 1) * rows]
            out = outs[near.index((dx, low))]
            out[...] = (fold(piece) if dx or low else piece).astype(out.dtype)
    lines = [ref[:, columns(0, width)] for ref in (master, moment, second)]
    weights = lines[0].astype(BF16).astype(F32)
    lines[:1] = [weights, lines[0] - weights]
    lines += [master[:, columns(dx, width)] for dx in range(1, reps)]
    state_ref[...] = fold(jnp.concatenate(lines, axis=0)).astype(BF16)


def join(refs, rows):
    return jnp.concatenate([unfold(ref[...].astype(F32), rows) for ref in refs], axis=0)


def join_body(rows, mine, other, *refs):
    out = refs[-1]
    both = join([mine, other], rows)
    out[...] = (both if out.shape == both.shape else fold(both)).astype(BF16)


def add(refs):
    return sum(ref[...].astype(F32) for ref in refs)


def plane_body(count, *refs):
    ins, (keep, send) = refs[:count], refs[-2:]
    total = ins[0][...]
    for ref in ins[1:]:
        total = total + unfold(ref[...].astype(F32), total.shape[0])
    half = total.shape[0] // 2
    keep[...] = total[:half]
    send[...] = fold(total[half:]).astype(BF16)


def halve_body(mine, other, *outs):
    total = mine[...] + unfold(other[...].astype(F32), mine.shape[0])
    if len(outs) == 1:
        outs[0][...] = fold(total).astype(BF16)
    else:
        half = total.shape[0] // 2
        outs[0][...] = total[:half]
        outs[1][...] = fold(total[half:]).astype(BF16)


def is_second():
    return lax.axis_index("high") >= lax.axis_size("high") // 2


def arrange_body(reps, per, state, state_other, *refs):
    out, old = refs[-2:]
    mine, other = (unfold(ref[...].astype(F32), (reps + 3) * per) for ref in (state, state_other))
    first, second = jnp.where(is_second(), other, mine), jnp.where(is_second(), mine, other)
    lines = [
        jnp.concatenate([block[i * per : (i + 1) * per] for block in (first, second)], axis=0)
        for i in range(reps + 3)
    ]
    out[0] = lines[0] + lines[1]
    out[1] = lines[2]
    out[2] = lines[3]
    here, parts = lax.axis_index("rep"), [lines[0], *lines[4:]]
    rows = []
    for rep in range(reps):
        piece = parts[rep]
        for at in range(1, reps):
            piece = jnp.where(here == at, parts[rep ^ at], piece)
        rows.append(piece)
    old[...] = fold(jnp.concatenate(rows, axis=1)).astype(BF16)


def adam_update(master, moment, second, gradient):
    moment_new = 0.9 * moment + 0.1 * gradient
    second_new = 0.95 * second + 0.05 * gradient * gradient
    first_fix = moment_new / (1.0 - 0.9**10)
    second_fix = second_new / (1.0 - 0.95**10)
    master_new = master - 0.01 * (first_fix / (jnp.sqrt(second_fix) + 1e-08) + 0.1 * master)
    return (master_new, moment_new, second_new)


def own_body(factor, per, mine, other, state, grad_ref, new_ref):
    g = unfold(add([mine, other]), 2 * per) * factor
    g = g.astype(BF16).astype(F32)
    new_ref[...] = fold(adam_update(state[0], state[1], state[2], g)[0]).astype(BF16)
    grad_ref[...] = jnp.where(is_second(), g[per:], g[:per]).astype(BF16)


def across_body(reps, near, *refs):
    *ins, new = refs[-len(near) - 1 :]
    width = new.shape[1] // reps
    for dx in range(reps):
        pieces = [ins[near.index((dx, low))] for low in range(LOW)]
        new[:, columns(dx, width)] = join(pieces, new.shape[0] // LOW).astype(BF16)


def wide_body(*refs):
    *ins, out = refs
    for dx, ref in enumerate(ins):
        out[:, columns(dx, ref.shape[1])] = ref[...].astype(F32)


def product_body(per, high, old, old_other, cot, gradient, master, moment, second, grad, *states):
    both = jnp.concatenate([old[...], old_other[...]], axis=0)
    rows = dot(both, cot[...], 1, 1).astype(BF16)
    for ref, value in zip(states, adam_update(master[...], moment[...], second[...], gradient[...])):
        ref[...] = value
    grad[...] = dot(one_hot(grad.shape[0], per, high), rows, 0, 0).astype(BF16)


def last_body(per, high, new, new_other, *refs):
    held, outs, (out, sems) = refs[:4], refs[4:9], refs[9:]
    copies = [pltpu.make_async_copy(a, b, sems.at[i]) for i, (a, b) in enumerate(zip(held, outs[1:]))]
    for copy in copies:
        copy.start()
    move = one_hot(out.shape[0], per, high)
    tile = out.shape[1] // OUT_COPIES
    half = new.shape[0]
    for i in range(OUT_COPIES):
        cols = pl.ds(i * tile, tile)
        chunk = dot(move[:half], new[:, cols], 0, 0) + dot(move[half:], new_other[:, cols], 0, 0)
        out[:, cols] = chunk.astype(BF16)
        copies.append(pltpu.make_async_copy(out.at[:, cols], outs[0].at[:, cols], sems.at[4 + i]))
        copies[-1].start()
    for copy in copies:
        copy.wait()


def local(hidden, cotangent, master, moment, second):
    reps, high = lax.axis_size("rep"), lax.axis_size("high")
    shards = high * LOW * CORES
    per, width = master.shape
    rows, part, tokens = shards * per, width // reps, hidden.shape[0]
    block = high * per
    factor = 1.0 / math.sqrt(tokens * reps * shards)
    far = [1 << i for i in range(high.bit_length() - 1)]
    halved, last = far[:-1], far[-1]
    near = sorted(((dx, low) for dx in range(reps) for low in range(LOW)),
                  key=lambda c: (c != (0, 0), -bool(c[0]) - bool(c[1]), c))
    states = (master, moment, second)

    ins = [pltpu.with_memory_space_constraint(x, pltpu.HBM) for x in (hidden.T, cotangent)]
    keep, send, cot = call(
        functools.partial(partial_body, per, high),
        [((rows // 2, width), F32), ((rows // 2, width), BF16), (cotangent.shape, BF16)],
        "partial", ins,
        cost=2 * rows * width * tokens,
        in_specs=[pl.BlockSpec(memory_space=pltpu.HBM)] * 2,
        scratch_shapes=[pltpu.VMEM((rows, tokens), BF16), pltpu.SemaphoreType.DMA((COT_COPIES * ROW_COPIES + 1,))],
    )

    recv = swap(send, 0, 0, 1)
    *pieces, state = call(
        functools.partial(middle_body, reps, near),
        [*((folded(block, part), BF16) if i else ((block, part), F32) for i in range(len(near))),
         (folded((reps + 3) * per, part), BF16)],
        "middle", [keep, recv, *states],
    )
    pieces = [pieces[0]] + [swap(p, dx, low) for p, (dx, low) in zip(pieces[1:], near[1:])]
    state_other = swap(state, 0, last * LOW)
    lines = block // 2
    body = functools.partial(plane_body, len(near))
    for bits in halved:
        keep, send = call(body, [((lines, part), F32), (folded(lines, part), BF16)], "halve", pieces)
        pieces, body, lines = [keep, swap(send, 0, bits * LOW)], halve_body, lines // 2
    (total,) = call(halve_body, [(folded(2 * per, part), BF16)], "whole", pieces)
    other = swap(total, 0, last * LOW)
    state, old = call(
        functools.partial(arrange_body, reps, per),
        [((3, 2 * per, part), F32), (folded(2 * per, width), BF16)],
        "arrange", [state, state_other, total],
    )
    grad, new = call(
        functools.partial(own_body, factor, per), [((per, part), BF16), (folded(2 * per, part), BF16)],
        "own", [total, other, state], cost=MAIN,
    )

    lines = 2 * per
    for bits in reversed(halved):
        body = functools.partial(join_body, lines)
        lines *= 2
        (new,) = call(body, [(folded(lines, part), BF16)], "copies", [new, swap(new, 0, bits * LOW)], cost=MAIN)
    grads = [grad] + [swap(grad, dx, 0) for dx in range(1, reps)]
    lines = 2 * per
    for chip in [bits * LOW for bits in reversed(halved)] + [1]:
        old_other = swap(old, 0, chip)
        shape = (2 * lines, width) if chip == 1 else folded(2 * lines, width)
        (old,) = call(functools.partial(join_body, lines), [(shape, BF16)], "join_old",
                      [old, old_other] + ([] if chip == 1 else [grad]))
        lines *= 2
    old_other = swap(old, 0, 0, 1)
    pieces = [swap(new, *c) if any(c) else new for c in near]
    (new,) = call(functools.partial(across_body, reps, near), [((rows // 2, width), BF16)],
                  "across", [old, *pieces])
    new_other = swap(new, 0, 0, 1)
    (grad,) = call(wide_body, [((per, width), F32)], "gradient", grads, cost=MAIN)
    outs = [((rows, tokens), BF16), *[((per, width), F32)] * 3]
    held = call(functools.partial(product_body, per, high), outs, "product",
                [old, old_other, cot, grad, *states], cost=2 * rows * width * tokens)
    outs = [((rows, width), BF16), *outs]
    updated, input_grad, *states = call(
        functools.partial(last_body, per, high), outs, "last", [new, new_other, *held],
        out_specs=(pl.BlockSpec(memory_space=pltpu.HBM),) * 5,
        scratch_shapes=[pltpu.VMEM(*outs[0]), pltpu.SemaphoreType.DMA((4 + OUT_COPIES,))],
    )
    return (input_grad.T, *states, updated)


def solution(mesh):
    reps, shards = mesh.shape["rep"], mesh.shape["shard"]
    split = Mesh(mesh.devices.reshape(reps, shards // LOW // CORES, LOW, CORES), (*CHIPS, "core"))
    by_row = P(("high", "low", "core"), None)
    by_token = P((*CHIPS, "core"), None)
    return jax.shard_map(
        local,
        mesh=split,
        in_specs=(by_token, by_token, by_row, by_row, by_row),
        out_specs=(by_token, by_row, by_row, by_row, P()),
        check_vma=False,
    )
```

```python
import functools
import math

import jax
import jax.numpy as jnp
from jax import lax
from jax.experimental import pallas as pl
from jax.experimental.pallas import tpu as pltpu
from jax.sharding import Mesh, PartitionSpec as P

F32 = jnp.float32
BF16 = jnp.bfloat16
VMEM = pl.BlockSpec(memory_space=pltpu.VMEM)
CORES = 2
LOW = 2
COT_COPIES = 2
OUT_COPIES = 5
MAIN = 3 * 10**9
CHIPS = ("rep", "high", "low")


def call(body, outs, name, ins, cost=1_000_000, **more):
    more = {"in_specs": [VMEM] * len(ins), "out_specs": (VMEM,) * len(outs), **more}
    return pl.pallas_call(
        body,
        out_shape=tuple(jax.ShapeDtypeStruct(*out) for out in outs),
        name=name,
        cost_estimate=pl.CostEstimate(flops=cost, bytes_accessed=1_000_000, transcendentals=0),
        compiler_params=pltpu.CompilerParams(vmem_limit_bytes=16 * 2**20),
        **more,
    )(*ins)


def parity(bits, chips):
    total = 0
    for i in range(chips.bit_length() - 1):
        total = total ^ ((bits >> i) & 1)
    return total


def swap(value, rep, chip, core=0):
    chips = lax.axis_size("high") * LOW
    bits = (rep * chips + chip) * CORES + (core ^ parity(chip, chips))
    count = lax.axis_size("rep") * chips * CORES
    return lax.ppermute(value, (*CHIPS, "core"), [(i, i ^ bits) for i in range(count)])


def one_hot(rows, per, high):
    at = lax.broadcasted_iota(jnp.int32, (rows, rows), 0)
    block = jnp.floor((at.astype(F32) + 0.5) * (1.0 / per)).astype(jnp.int32)
    chips = high * LOW
    low, here = lax.axis_index("low"), lax.axis_index("high")
    last = high.bit_length() - 2
    far = (block & 1) << last
    for i in range(last):
        far = far | ((((block >> (last - i)) & 1) ^ ((here >> i) & 1)) << i)
    chip = far * LOW + (low ^ ((block & (chips - 1)) // high))
    other = parity(chip ^ (here * LOW + low), chips)
    core = lax.axis_index("core") ^ (block // chips) ^ other
    source = (chip * CORES + core) * per + at - block * per
    return (lax.broadcasted_iota(jnp.int32, (rows, rows), 1) == source).astype(BF16)


def dot(a, b, ca, cb):
    return lax.dot_general(a, b, (((ca,), (cb,)), ((), ())), preferred_element_type=F32)


def columns(dx, width):
    return pl.ds(pl.multiple_of((lax.axis_index("rep") ^ dx) * width, 128), width)


def folds(rows, width):
    some = [f for f in range(1, 9) if width % (128 * f) == 0]
    return min(some, key=lambda f: (-(-rows * f // 8) * 8 * (width // f), f))


def folded(rows, width):
    f = folds(rows, width)
    return (rows * f, width // f)


def fold(value):
    f = folds(*value.shape)
    width = value.shape[1] // f
    return jnp.concatenate([value[:, i * width : (i + 1) * width] for i in range(f)], axis=0)


def unfold(value, rows):
    f = value.shape[0] // rows
    return jnp.concatenate([value[i * rows : (i + 1) * rows] for i in range(f)], axis=1)


def partial_body(per, high, hid_hbm, cot_hbm, keep_ref, send_ref, cot_ref, hid, sems):
    rows, width = hid.shape[0], cot_ref.shape[1]
    tile = width // COT_COPIES
    pieces = [(hid_hbm, hid)]
    pieces += [
        (cot_hbm.at[:, pl.ds(i * tile, tile)], cot_ref.at[:, pl.ds(i * tile, tile)])
        for i in range(COT_COPIES)
    ]
    copies = [pltpu.make_async_copy(a, b, sems.at[i]) for i, (a, b) in enumerate(pieces)]
    for copy in copies:
        copy.start()
    move = one_hot(rows, per, high)
    copies[0].wait()
    moved = dot(move, hid[...], 1, 0).astype(BF16)
    for i in range(COT_COPIES):
        copies[1 + i].wait()
        cols = pl.ds(i * tile, tile)
        g = dot(moved, cot_ref[:, cols], 1, 0)
        keep_ref[:, cols] = g[: rows // 2]
        send_ref[:, cols] = g[rows // 2 :].astype(BF16)


def middle_body(reps, near, keep_ref, recv_ref, master, moment, second, *outs):
    *outs, state_ref = outs
    width = keep_ref.shape[1] // reps
    rows = keep_ref.shape[0] // LOW
    for dx in range(reps):
        cols = columns(dx, width)
        total = keep_ref[:, cols] + recv_ref[:, cols].astype(F32)
        for low in range(LOW):
            piece = total[low * rows : (low + 1) * rows]
            out = outs[near.index((dx, low))]
            out[...] = (fold(piece) if dx or low else piece).astype(out.dtype)
    lines = [ref[:, columns(0, width)] for ref in (master, moment, second)]
    weights = lines[0].astype(BF16).astype(F32)
    lines[:1] = [weights, lines[0] - weights]
    lines += [master[:, columns(dx, width)] for dx in range(1, reps)]
    state_ref[...] = fold(jnp.concatenate(lines, axis=0)).astype(BF16)


def join(refs, rows):
    return jnp.concatenate([unfold(ref[...].astype(F32), rows) for ref in refs], axis=0)


def join_body(rows, mine, other, *refs):
    out = refs[-1]
    both = join([mine, other], rows)
    out[...] = (both if out.shape == both.shape else fold(both)).astype(BF16)


def add(refs):
    return sum(ref[...].astype(F32) for ref in refs)


def plane_body(count, *refs):
    ins, (keep, send) = refs[:count], refs[-2:]
    total = ins[0][...]
    for ref in ins[1:]:
        total = total + unfold(ref[...].astype(F32), total.shape[0])
    half = total.shape[0] // 2
    keep[...] = total[:half]
    send[...] = fold(total[half:]).astype(BF16)


def halve_body(mine, other, *outs):
    total = mine[...] + unfold(other[...].astype(F32), mine.shape[0])
    if len(outs) == 1:
        outs[0][...] = fold(total).astype(BF16)
    else:
        half = total.shape[0] // 2
        outs[0][...] = total[:half]
        outs[1][...] = fold(total[half:]).astype(BF16)


def is_second():
    return lax.axis_index("high") >= lax.axis_size("high") // 2


def arrange_body(reps, per, state, state_other, *refs):
    out, old = refs[-2:]
    mine, other = (unfold(ref[...].astype(F32), (reps + 3) * per) for ref in (state, state_other))
    first, second = jnp.where(is_second(), other, mine), jnp.where(is_second(), mine, other)
    lines = [
        jnp.concatenate([block[i * per : (i + 1) * per] for block in (first, second)], axis=0)
        for i in range(reps + 3)
    ]
    out[0] = lines[0] + lines[1]
    out[1] = lines[2]
    out[2] = lines[3]
    here, parts = lax.axis_index("rep"), [lines[0], *lines[4:]]
    rows = []
    for rep in range(reps):
        piece = parts[rep]
        for at in range(1, reps):
            piece = jnp.where(here == at, parts[rep ^ at], piece)
        rows.append(piece)
    old[...] = fold(jnp.concatenate(rows, axis=1)).astype(BF16)


def adam_update(master, moment, second, gradient):
    moment_new = 0.9 * moment + 0.1 * gradient
    second_new = 0.95 * second + 0.05 * gradient * gradient
    first_fix = moment_new / (1.0 - 0.9**10)
    second_fix = second_new / (1.0 - 0.95**10)
    master_new = master - 0.01 * (first_fix / (jnp.sqrt(second_fix) + 1e-08) + 0.1 * master)
    return (master_new, moment_new, second_new)


def own_body(factor, per, mine, other, state, grad_ref, new_ref):
    g = unfold(add([mine, other]), 2 * per) * factor
    g = g.astype(BF16).astype(F32)
    new_ref[...] = fold(adam_update(state[0], state[1], state[2], g)[0]).astype(BF16)
    grad_ref[...] = jnp.where(is_second(), g[per:], g[:per]).astype(BF16)


def across_body(reps, near, *refs):
    *ins, new = refs[-len(near) - 1 :]
    width = new.shape[1] // reps
    for dx in range(reps):
        pieces = [ins[near.index((dx, low))] for low in range(LOW)]
        new[:, columns(dx, width)] = join(pieces, new.shape[0] // LOW).astype(BF16)


def wide_body(*refs):
    *ins, out = refs
    for dx, ref in enumerate(ins):
        out[:, columns(dx, ref.shape[1])] = ref[...].astype(F32)


def product_body(per, high, old, old_other, cot, gradient, master, moment, second, grad, *states):
    both = jnp.concatenate([old[...], old_other[...]], axis=0)
    rows = dot(both, cot[...], 1, 1).astype(BF16)
    for ref, value in zip(states, adam_update(master[...], moment[...], second[...], gradient[...])):
        ref[...] = value
    grad[...] = dot(one_hot(grad.shape[0], per, high), rows, 0, 0).astype(BF16)


def last_body(per, high, new, new_other, *refs):
    held, outs, (out, sems) = refs[:4], refs[4:9], refs[9:]
    copies = [pltpu.make_async_copy(a, b, sems.at[i]) for i, (a, b) in enumerate(zip(held, outs[1:]))]
    for copy in copies:
        copy.start()
    move = one_hot(out.shape[0], per, high)
    tile = out.shape[1] // OUT_COPIES
    half = new.shape[0]
    for i in range(OUT_COPIES):
        cols = pl.ds(i * tile, tile)
        chunk = dot(move[:half], new[:, cols], 0, 0) + dot(move[half:], new_other[:, cols], 0, 0)
        out[:, cols] = chunk.astype(BF16)
        copies.append(pltpu.make_async_copy(out.at[:, cols], outs[0].at[:, cols], sems.at[4 + i]))
        copies[-1].start()
    for copy in copies:
        copy.wait()


def local(hidden, cotangent, master, moment, second):
    reps, high = lax.axis_size("rep"), lax.axis_size("high")
    shards = high * LOW * CORES
    per, width = master.shape
    rows, part, tokens = shards * per, width // reps, hidden.shape[0]
    block = high * per
    factor = 1.0 / math.sqrt(tokens * reps * shards)
    far = [1 << i for i in range(high.bit_length() - 1)]
    halved, last = far[:-1], far[-1]
    near = sorted(((dx, low) for dx in range(reps) for low in range(LOW)),
                  key=lambda c: (c != (0, 0), -bool(c[0]) - bool(c[1]), c[::-1]))
    states = (master, moment, second)

    ins = [pltpu.with_memory_space_constraint(x, pltpu.HBM) for x in (hidden.T, cotangent)]
    keep, send, cot = call(
        functools.partial(partial_body, per, high),
        [((rows // 2, width), F32), ((rows // 2, width), BF16), (cotangent.shape, BF16)],
        "partial", ins,
        cost=2 * rows * width * tokens,
        in_specs=[pl.BlockSpec(memory_space=pltpu.HBM)] * 2,
        scratch_shapes=[pltpu.VMEM((rows, tokens), BF16), pltpu.SemaphoreType.DMA((COT_COPIES + 1,))],
    )

    recv = swap(send, 0, 0, 1)
    *pieces, state = call(
        functools.partial(middle_body, reps, near),
        [*((folded(block, part), BF16) if i else ((block, part), F32) for i in range(len(near))),
         (folded((reps + 3) * per, part), BF16)],
        "middle", [keep, recv, *states],
    )
    pieces = [pieces[0]] + [swap(p, dx, low) for p, (dx, low) in zip(pieces[1:], near[1:])]
    state_other = swap(state, 0, last * LOW)
    lines = block // 2
    body = functools.partial(plane_body, len(near))
    for bits in halved:
        keep, send = call(body, [((lines, part), F32), (folded(lines, part), BF16)], "halve", pieces)
        pieces, body, lines = [keep, swap(send, 0, bits * LOW)], halve_body, lines // 2
    (total,) = call(halve_body, [(folded(2 * per, part), BF16)], "whole", pieces)
    other = swap(total, 0, last * LOW)
    state, old = call(
        functools.partial(arrange_body, reps, per),
        [((3, 2 * per, part), F32), (folded(2 * per, width), BF16)],
        "arrange", [state, state_other, total],
    )
    grad, new = call(
        functools.partial(own_body, factor, per), [((per, part), BF16), (folded(2 * per, part), BF16)],
        "own", [total, other, state], cost=MAIN,
    )

    lines = 2 * per
    for bits in reversed(halved):
        body = functools.partial(join_body, lines)
        lines *= 2
        (new,) = call(body, [(folded(lines, part), BF16)], "copies", [new, swap(new, 0, bits * LOW)], cost=MAIN)
    grads = [grad] + [swap(grad, dx, 0) for dx in range(1, reps)]
    lines = 2 * per
    for chip in [bits * LOW for bits in reversed(halved)] + [1]:
        old_other = swap(old, 0, chip)
        shape = (2 * lines, width) if chip == 1 else folded(2 * lines, width)
        (old,) = call(functools.partial(join_body, lines), [(shape, BF16)], "join_old",
                      [old, old_other] + ([] if chip == 1 else [grad]))
        lines *= 2
    old_other = swap(old, 0, 0, 1)
    pieces = [swap(new, *c) if any(c) else new for c in near]
    (new,) = call(functools.partial(across_body, reps, near), [((rows // 2, width), BF16)],
                  "across", [old, *pieces])
    new_other = swap(new, 0, 0, 1)
    (grad,) = call(wide_body, [((per, width), F32)], "gradient", grads, cost=MAIN)
    outs = [((rows, tokens), BF16), *[((per, width), F32)] * 3]
    held = call(functools.partial(product_body, per, high), outs, "product",
                [old, old_other, cot, grad, *states], cost=2 * rows * width * tokens)
    outs = [((rows, width), BF16), *outs]
    updated, input_grad, *states = call(
        functools.partial(last_body, per, high), outs, "last", [new, new_other, *held],
        out_specs=(pl.BlockSpec(memory_space=pltpu.HBM),) * 5,
        scratch_shapes=[pltpu.VMEM(*outs[0]), pltpu.SemaphoreType.DMA((4 + OUT_COPIES,))],
    )
    return (input_grad.T, *states, updated)


def solution(mesh):
    reps, shards = mesh.shape["rep"], mesh.shape["shard"]
    split = Mesh(mesh.devices.reshape(reps, shards // LOW // CORES, LOW, CORES), (*CHIPS, "core"))
    by_row = P(("high", "low", "core"), None)
    by_token = P((*CHIPS, "core"), None)
    return jax.shard_map(
        local,
        mesh=split,
        in_specs=(by_token, by_token, by_row, by_row, by_row),
        out_specs=(by_token, by_row, by_row, by_row, P()),
        check_vma=False,
    )
```

```python
import functools
import math

import jax
import jax.numpy as jnp
from jax import lax
from jax.experimental import pallas as pl
from jax.experimental.pallas import tpu as pltpu
from jax.sharding import Mesh, PartitionSpec as P

F32 = jnp.float32
BF16 = jnp.bfloat16
VMEM = pl.BlockSpec(memory_space=pltpu.VMEM)
CORES = 2
LOW = 2
COT_COPIES = 2
OUT_COPIES = 5
MAIN = 3 * 10**9
CHIPS = ("rep", "high", "low")


def call(body, outs, name, ins, cost=1_000_000, **more):
    more = {"in_specs": [VMEM] * len(ins), "out_specs": (VMEM,) * len(outs), **more}
    return pl.pallas_call(
        body,
        out_shape=tuple(jax.ShapeDtypeStruct(*out) for out in outs),
        name=name,
        cost_estimate=pl.CostEstimate(flops=cost, bytes_accessed=1_000_000, transcendentals=0),
        compiler_params=pltpu.CompilerParams(vmem_limit_bytes=16 * 2**20),
        **more,
    )(*ins)


def parity(bits, chips):
    total = 0
    for i in range(chips.bit_length() - 1):
        total = total ^ ((bits >> i) & 1)
    return total


def swap(value, rep, chip, core=0):
    chips = lax.axis_size("high") * LOW
    bits = (rep * chips + chip) * CORES + (core ^ parity(chip, chips))
    count = lax.axis_size("rep") * chips * CORES
    return lax.ppermute(value, (*CHIPS, "core"), [(i, i ^ bits) for i in range(count)])


def one_hot(rows, per, high):
    at = lax.broadcasted_iota(jnp.int32, (rows, rows), 0)
    block = jnp.floor((at.astype(F32) + 0.5) * (1.0 / per)).astype(jnp.int32)
    chips = high * LOW
    low, here = lax.axis_index("low"), lax.axis_index("high")
    last = high.bit_length() - 2
    far = (block & 1) << last
    for i in range(last):
        far = far | ((((block >> (last - i)) & 1) ^ ((here >> i) & 1)) << i)
    chip = far * LOW + (low ^ ((block & (chips - 1)) // high))
    other = parity(chip ^ (here * LOW + low), chips)
    core = lax.axis_index("core") ^ (block // chips) ^ other
    source = (chip * CORES + core) * per + at - block * per
    return (lax.broadcasted_iota(jnp.int32, (rows, rows), 1) == source).astype(BF16)


def dot(a, b, ca, cb):
    return lax.dot_general(a, b, (((ca,), (cb,)), ((), ())), preferred_element_type=F32)


def columns(dx, width):
    return pl.ds(pl.multiple_of((lax.axis_index("rep") ^ dx) * width, 128), width)


def folds(rows, width):
    some = [f for f in range(1, 9) if width % (128 * f) == 0]
    return min(some, key=lambda f: (-(-rows * f // 8) * 8 * (width // f), f))


def folded(rows, width):
    f = folds(rows, width)
    return (rows * f, width // f)


def fold(value):
    f = folds(*value.shape)
    width = value.shape[1] // f
    return jnp.concatenate([value[:, i * width : (i + 1) * width] for i in range(f)], axis=0)


def unfold(value, rows):
    f = value.shape[0] // rows
    return jnp.concatenate([value[i * rows : (i + 1) * rows] for i in range(f)], axis=1)


def partial_body(per, high, hid_hbm, cot_hbm, keep_ref, send_ref, cot_ref, hid, sems):
    rows, width = hid.shape[0], cot_ref.shape[1]
    tile = width // COT_COPIES
    pieces = [(hid_hbm, hid)]
    pieces += [
        (cot_hbm.at[:, pl.ds(i * tile, tile)], cot_ref.at[:, pl.ds(i * tile, tile)])
        for i in range(COT_COPIES)
    ]
    copies = [pltpu.make_async_copy(a, b, sems.at[i]) for i, (a, b) in enumerate(pieces)]
    for copy in copies:
        copy.start()
    move = one_hot(rows, per, high)
    copies[0].wait()
    moved = dot(move, hid[...], 1, 0).astype(BF16)
    for i in range(COT_COPIES):
        copies[1 + i].wait()
        cols = pl.ds(i * tile, tile)
        g = dot(moved, cot_ref[:, cols], 1, 0)
        keep_ref[:, cols] = g[: rows // 2]
        send_ref[:, cols] = g[rows // 2 :].astype(BF16)


def middle_body(reps, near, keep_ref, recv_ref, master, moment, second, *outs):
    *outs, state_ref = outs
    width = keep_ref.shape[1] // reps
    rows = keep_ref.shape[0] // LOW
    for dx in range(reps):
        cols = columns(dx, width)
        total = keep_ref[:, cols] + recv_ref[:, cols].astype(F32)
        for low in range(LOW):
            piece = total[low * rows : (low + 1) * rows]
            out = outs[near.index((dx, low))]
            out[...] = (fold(piece) if dx or low else piece).astype(out.dtype)
    lines = [ref[:, columns(0, width)] for ref in (master, moment, second)]
    weights = lines[0].astype(BF16).astype(F32)
    lines[:1] = [weights, lines[0] - weights]
    lines += [master[:, columns(dx, width)] for dx in range(1, reps)]
    state_ref[...] = fold(jnp.concatenate(lines, axis=0)).astype(BF16)


def join(refs, rows):
    return jnp.concatenate([unfold(ref[...].astype(F32), rows) for ref in refs], axis=0)


def join_body(rows, mine, other, *refs):
    out = refs[-1]
    both = join([mine, other], rows)
    out[...] = (both if out.shape == both.shape else fold(both)).astype(BF16)


def add(refs):
    return sum(ref[...].astype(F32) for ref in refs)


def plane_body(count, *refs):
    ins, (keep, send) = refs[:count], refs[-2:]
    total = ins[0][...]
    for ref in ins[1:]:
        total = total + unfold(ref[...].astype(F32), total.shape[0])
    half = total.shape[0] // 2
    keep[...] = total[:half]
    send[...] = fold(total[half:]).astype(BF16)


def halve_body(mine, other, *outs):
    total = mine[...] + unfold(other[...].astype(F32), mine.shape[0])
    if len(outs) == 1:
        outs[0][...] = fold(total).astype(BF16)
    else:
        half = total.shape[0] // 2
        outs[0][...] = total[:half]
        outs[1][...] = fold(total[half:]).astype(BF16)


def is_second():
    return lax.axis_index("high") >= lax.axis_size("high") // 2


def arrange_body(reps, per, state, state_other, *refs):
    out, old = refs[-2:]
    mine, other = (unfold(ref[...].astype(F32), (reps + 3) * per) for ref in (state, state_other))
    first, second = jnp.where(is_second(), other, mine), jnp.where(is_second(), mine, other)
    lines = [
        jnp.concatenate([block[i * per : (i + 1) * per] for block in (first, second)], axis=0)
        for i in range(reps + 3)
    ]
    out[0] = lines[0] + lines[1]
    out[1] = lines[2]
    out[2] = lines[3]
    here, parts = lax.axis_index("rep"), [lines[0], *lines[4:]]
    rows = []
    for rep in range(reps):
        piece = parts[rep]
        for at in range(1, reps):
            piece = jnp.where(here == at, parts[rep ^ at], piece)
        rows.append(piece)
    old[...] = fold(jnp.concatenate(rows, axis=1)).astype(BF16)


def adam_update(master, moment, second, gradient):
    moment_new = 0.9 * moment + 0.1 * gradient
    second_new = 0.95 * second + 0.05 * gradient * gradient
    first_fix = moment_new / (1.0 - 0.9**10)
    second_fix = second_new / (1.0 - 0.95**10)
    master_new = master - 0.01 * (first_fix / (jnp.sqrt(second_fix) + 1e-08) + 0.1 * master)
    return (master_new, moment_new, second_new)


def own_body(factor, per, mine, other, state, grad_ref, new_ref):
    g = unfold(add([mine, other]), 2 * per) * factor
    g = g.astype(BF16).astype(F32)
    new_ref[...] = fold(adam_update(state[0], state[1], state[2], g)[0]).astype(BF16)
    grad_ref[...] = jnp.where(is_second(), g[per:], g[:per]).astype(BF16)


def across_body(reps, near, *refs):
    *ins, new = refs[-len(near) - 1 :]
    width = new.shape[1] // reps
    for dx in range(reps):
        pieces = [ins[near.index((dx, low))] for low in range(LOW)]
        new[:, columns(dx, width)] = join(pieces, new.shape[0] // LOW).astype(BF16)


def wide_body(*refs):
    *ins, out = refs
    for dx, ref in enumerate(ins):
        out[:, columns(dx, ref.shape[1])] = ref[...].astype(F32)


def product_body(per, high, old, old_other, cot, gradient, master, moment, second, grad, *states):
    both = jnp.concatenate([old[...], old_other[...]], axis=0)
    rows = dot(both, cot[...], 1, 1).astype(BF16)
    for ref, value in zip(states, adam_update(master[...], moment[...], second[...], gradient[...])):
        ref[...] = value
    grad[...] = dot(one_hot(grad.shape[0], per, high), rows, 0, 0).astype(BF16)


def last_body(per, high, new, new_other, *refs):
    held, outs, (out, sems) = refs[:4], refs[4:9], refs[9:]
    copies = []
    move = one_hot(out.shape[0], per, high)
    tile = out.shape[1] // OUT_COPIES
    half = new.shape[0]
    for i in range(OUT_COPIES):
        cols = pl.ds(i * tile, tile)
        chunk = dot(move[:half], new[:, cols], 0, 0) + dot(move[half:], new_other[:, cols], 0, 0)
        out[:, cols] = chunk.astype(BF16)
        copies.append(pltpu.make_async_copy(out.at[:, cols], outs[0].at[:, cols], sems.at[4 + i]))
        copies[-1].start()
        if i < len(held):
            copies.append(pltpu.make_async_copy(held[i], outs[1 + i], sems.at[i]))
            copies[-1].start()
    for copy in copies:
        copy.wait()


def local(hidden, cotangent, master, moment, second):
    reps, high = lax.axis_size("rep"), lax.axis_size("high")
    shards = high * LOW * CORES
    per, width = master.shape
    rows, part, tokens = shards * per, width // reps, hidden.shape[0]
    block = high * per
    factor = 1.0 / math.sqrt(tokens * reps * shards)
    far = [1 << i for i in range(high.bit_length() - 1)]
    halved, last = far[:-1], far[-1]
    near = sorted(((dx, low) for dx in range(reps) for low in range(LOW)),
                  key=lambda c: (c != (0, 0), -bool(c[0]) - bool(c[1]), c[::-1]))
    states = (master, moment, second)

    ins = [pltpu.with_memory_space_constraint(x, pltpu.HBM) for x in (hidden.T, cotangent)]
    keep, send, cot = call(
        functools.partial(partial_body, per, high),
        [((rows // 2, width), F32), ((rows // 2, width), BF16), (cotangent.shape, BF16)],
        "partial", ins,
        cost=2 * rows * width * tokens,
        in_specs=[pl.BlockSpec(memory_space=pltpu.HBM)] * 2,
        scratch_shapes=[pltpu.VMEM((rows, tokens), BF16), pltpu.SemaphoreType.DMA((COT_COPIES + 1,))],
    )

    recv = swap(send, 0, 0, 1)
    *pieces, state = call(
        functools.partial(middle_body, reps, near),
        [*((folded(block, part), BF16) if i else ((block, part), F32) for i in range(len(near))),
         (folded((reps + 3) * per, part), BF16)],
        "middle", [keep, recv, *states],
    )
    pieces = [pieces[0]] + [swap(p, dx, low) for p, (dx, low) in zip(pieces[1:], near[1:])]
    state_other = swap(state, 0, last * LOW)
    lines = block // 2
    body = functools.partial(plane_body, len(near))
    for bits in halved:
        keep, send = call(body, [((lines, part), F32), (folded(lines, part), BF16)], "halve", pieces)
        pieces, body, lines = [keep, swap(send, 0, bits * LOW)], halve_body, lines // 2
    (total,) = call(halve_body, [(folded(2 * per, part), BF16)], "whole", pieces)
    other = swap(total, 0, last * LOW)
    state, old = call(
        functools.partial(arrange_body, reps, per),
        [((3, 2 * per, part), F32), (folded(2 * per, width), BF16)],
        "arrange", [state, state_other, total],
    )
    grad, new = call(
        functools.partial(own_body, factor, per), [((per, part), BF16), (folded(2 * per, part), BF16)],
        "own", [total, other, state], cost=MAIN,
    )

    lines = 2 * per
    for bits in reversed(halved):
        body = functools.partial(join_body, lines)
        lines *= 2
        (new,) = call(body, [(folded(lines, part), BF16)], "copies", [new, swap(new, 0, bits * LOW)], cost=MAIN)
    grads = [grad] + [swap(grad, dx, 0) for dx in range(1, reps)]
    lines = 2 * per
    for chip in [bits * LOW for bits in reversed(halved)] + [1]:
        old_other = swap(old, 0, chip)
        shape = (2 * lines, width) if chip == 1 else folded(2 * lines, width)
        (old,) = call(functools.partial(join_body, lines), [(shape, BF16)], "join_old",
                      [old, old_other] + ([] if chip == 1 else [grad]))
        lines *= 2
    old_other = swap(old, 0, 0, 1)
    pieces = [swap(new, *c) if any(c) else new for c in near]
    (new,) = call(functools.partial(across_body, reps, near), [((rows // 2, width), BF16)],
                  "across", [old, *pieces])
    new_other = swap(new, 0, 0, 1)
    (grad,) = call(wide_body, [((per, width), F32)], "gradient", grads, cost=MAIN)
    outs = [((rows, tokens), BF16), *[((per, width), F32)] * 3]
    held = call(functools.partial(product_body, per, high), outs, "product",
                [old, old_other, cot, grad, *states], cost=2 * rows * width * tokens)
    outs = [((rows, width), BF16), *outs]
    updated, input_grad, *states = call(
        functools.partial(last_body, per, high), outs, "last", [new, new_other, *held],
        out_specs=(pl.BlockSpec(memory_space=pltpu.HBM),) * 5,
        scratch_shapes=[pltpu.VMEM(*outs[0]), pltpu.SemaphoreType.DMA((4 + OUT_COPIES,))],
    )
    return (input_grad.T, *states, updated)


def solution(mesh):
    reps, shards = mesh.shape["rep"], mesh.shape["shard"]
    split = Mesh(mesh.devices.reshape(reps, shards // LOW // CORES, LOW, CORES), (*CHIPS, "core"))
    by_row = P(("high", "low", "core"), None)
    by_token = P((*CHIPS, "core"), None)
    return jax.shard_map(
        local,
        mesh=split,
        in_specs=(by_token, by_token, by_row, by_row, by_row),
        out_specs=(by_token, by_row, by_row, by_row, P()),
        check_vma=False,
    )
```

```python
import functools
import math

import jax
import jax.numpy as jnp
from jax import lax
from jax.experimental import pallas as pl
from jax.experimental.pallas import tpu as pltpu
from jax.sharding import Mesh, PartitionSpec as P

F32 = jnp.float32
BF16 = jnp.bfloat16
VMEM = pl.BlockSpec(memory_space=pltpu.VMEM)
CORES = 2
LOW = 2
COT_COPIES = 2
OUT_COPIES = 5
MAIN = 3 * 10**9
CHIPS = ("rep", "high", "low")


def call(body, outs, name, ins, cost=1_000_000, **more):
    more = {"in_specs": [VMEM] * len(ins), "out_specs": (VMEM,) * len(outs), **more}
    return pl.pallas_call(
        body,
        out_shape=tuple(jax.ShapeDtypeStruct(*out) for out in outs),
        name=name,
        cost_estimate=pl.CostEstimate(flops=cost, bytes_accessed=1_000_000, transcendentals=0),
        compiler_params=pltpu.CompilerParams(vmem_limit_bytes=16 * 2**20),
        **more,
    )(*ins)


def parity(bits, chips):
    total = 0
    for i in range(chips.bit_length() - 1):
        total = total ^ ((bits >> i) & 1)
    return total


def swap(value, rep, chip, core=0):
    chips = lax.axis_size("high") * LOW
    bits = (rep * chips + chip) * CORES + (core ^ parity(chip, chips))
    count = lax.axis_size("rep") * chips * CORES
    return lax.ppermute(value, (*CHIPS, "core"), [(i, i ^ bits) for i in range(count)])


def one_hot(rows, per, high):
    at = lax.broadcasted_iota(jnp.int32, (rows, rows), 0)
    block = jnp.floor((at.astype(F32) + 0.5) * (1.0 / per)).astype(jnp.int32)
    chips = high * LOW
    low, here = lax.axis_index("low"), lax.axis_index("high")
    last = high.bit_length() - 2
    far = (block & 1) << last
    for i in range(last):
        far = far | ((((block >> (last - i)) & 1) ^ ((here >> i) & 1)) << i)
    chip = far * LOW + (low ^ ((block & (chips - 1)) // high))
    other = parity(chip ^ (here * LOW + low), chips)
    core = lax.axis_index("core") ^ (block // chips) ^ other
    source = (chip * CORES + core) * per + at - block * per
    return (lax.broadcasted_iota(jnp.int32, (rows, rows), 1) == source).astype(BF16)


def dot(a, b, ca, cb):
    return lax.dot_general(a, b, (((ca,), (cb,)), ((), ())), preferred_element_type=F32)


def columns(dx, width):
    return pl.ds(pl.multiple_of((lax.axis_index("rep") ^ dx) * width, 128), width)


def folds(rows, width):
    some = [f for f in range(1, 9) if width % (128 * f) == 0]
    return min(some, key=lambda f: (-(-rows * f // 8) * 8 * (width // f), f))


def folded(rows, width):
    f = folds(rows, width)
    return (rows * f, width // f)


def fold(value):
    f = folds(*value.shape)
    width = value.shape[1] // f
    return jnp.concatenate([value[:, i * width : (i + 1) * width] for i in range(f)], axis=0)


def unfold(value, rows):
    f = value.shape[0] // rows
    return jnp.concatenate([value[i * rows : (i + 1) * rows] for i in range(f)], axis=1)


def partial_body(per, high, hid_hbm, cot_hbm, keep_ref, send_ref, cot_ref, hid, sems):
    rows, width = hid.shape[0], cot_ref.shape[1]
    tile = width // COT_COPIES
    pieces = [(hid_hbm, hid)]
    pieces += [
        (cot_hbm.at[:, pl.ds(i * tile, tile)], cot_ref.at[:, pl.ds(i * tile, tile)])
        for i in range(COT_COPIES)
    ]
    copies = [pltpu.make_async_copy(a, b, sems.at[i]) for i, (a, b) in enumerate(pieces)]
    for copy in copies:
        copy.start()
    move = one_hot(rows, per, high)
    copies[0].wait()
    moved = dot(move, hid[...], 1, 0).astype(BF16)
    for i in range(COT_COPIES):
        copies[1 + i].wait()
        cols = pl.ds(i * tile, tile)
        g = dot(moved, cot_ref[:, cols], 1, 0)
        keep_ref[:, cols] = g[: rows // 2]
        send_ref[:, cols] = g[rows // 2 :].astype(BF16)


def middle_body(reps, near, keep_ref, recv_ref, master, moment, second, *outs):
    *outs, state_ref = outs
    width = keep_ref.shape[1] // reps
    rows = keep_ref.shape[0] // LOW
    for dx in range(reps):
        cols = columns(dx, width)
        total = keep_ref[:, cols] + recv_ref[:, cols].astype(F32)
        for low in range(LOW):
            piece = total[low * rows : (low + 1) * rows]
            out = outs[near.index((dx, low))]
            out[...] = (fold(piece) if dx or low else piece).astype(out.dtype)
    lines = [ref[:, columns(0, width)] for ref in (master, moment, second)]
    weights = lines[0].astype(BF16).astype(F32)
    lines[:1] = [weights, lines[0] - weights]
    lines += [master[:, columns(dx, width)] for dx in range(1, reps)]
    state_ref[...] = fold(jnp.concatenate(lines, axis=0)).astype(BF16)


def join(refs, rows):
    return jnp.concatenate([unfold(ref[...].astype(F32), rows) for ref in refs], axis=0)


def join_body(rows, mine, other, *refs):
    out = refs[-1]
    both = join([mine, other], rows)
    out[...] = (both if out.shape == both.shape else fold(both)).astype(BF16)


def add(refs):
    return sum(ref[...].astype(F32) for ref in refs)


def plane_body(count, *refs):
    ins, (keep, send) = refs[:count], refs[-2:]
    total = ins[0][...]
    for ref in ins[1:]:
        total = total + unfold(ref[...].astype(F32), total.shape[0])
    half = total.shape[0] // 2
    keep[...] = total[:half]
    send[...] = fold(total[half:]).astype(BF16)


def halve_body(mine, other, *outs):
    total = mine[...] + unfold(other[...].astype(F32), mine.shape[0])
    if len(outs) == 1:
        outs[0][...] = fold(total).astype(BF16)
    else:
        half = total.shape[0] // 2
        outs[0][...] = total[:half]
        outs[1][...] = fold(total[half:]).astype(BF16)


def is_second():
    return lax.axis_index("high") >= lax.axis_size("high") // 2


def arrange_body(reps, per, state, state_other, *refs):
    out, old = refs[-2:]
    mine, other = (unfold(ref[...].astype(F32), (reps + 3) * per) for ref in (state, state_other))
    first, second = jnp.where(is_second(), other, mine), jnp.where(is_second(), mine, other)
    lines = [
        jnp.concatenate([block[i * per : (i + 1) * per] for block in (first, second)], axis=0)
        for i in range(reps + 3)
    ]
    out[0] = lines[0] + lines[1]
    out[1] = lines[2]
    out[2] = lines[3]
    here, parts = lax.axis_index("rep"), [lines[0], *lines[4:]]
    rows = []
    for rep in range(reps):
        piece = parts[rep]
        for at in range(1, reps):
            piece = jnp.where(here == at, parts[rep ^ at], piece)
        rows.append(piece)
    old[...] = fold(jnp.concatenate(rows, axis=1)).astype(BF16)


def adam_update(master, moment, second, gradient):
    moment_new = 0.9 * moment + 0.1 * gradient
    second_new = 0.95 * second + 0.05 * gradient * gradient
    first_fix = moment_new / (1.0 - 0.9**10)
    second_fix = second_new / (1.0 - 0.95**10)
    master_new = master - 0.01 * (first_fix / (jnp.sqrt(second_fix) + 1e-08) + 0.1 * master)
    return (master_new, moment_new, second_new)


def own_body(factor, per, mine, other, state, grad_ref, new_ref):
    g = unfold(add([mine, other]), 2 * per) * factor
    g = g.astype(BF16).astype(F32)
    new_ref[...] = fold(adam_update(state[0], state[1], state[2], g)[0]).astype(BF16)
    grad_ref[...] = jnp.where(is_second(), g[per:], g[:per]).astype(BF16)


def across_body(reps, near, *refs):
    *ins, new = refs[-len(near) - 1 :]
    width = new.shape[1] // reps
    for dx in range(reps):
        pieces = [ins[near.index((dx, low))] for low in range(LOW)]
        new[:, columns(dx, width)] = join(pieces, new.shape[0] // LOW).astype(BF16)


def wide_body(*refs):
    *ins, out = refs
    for dx, ref in enumerate(ins):
        out[:, columns(dx, ref.shape[1])] = ref[...].astype(F32)


def product_body(per, high, old, old_other, cot, gradient, master, moment, second, move, grad, *states):
    move[...] = one_hot(grad.shape[0], per, high)
    both = jnp.concatenate([old[...], old_other[...]], axis=0)
    rows = dot(both, cot[...], 1, 1).astype(BF16)
    for ref, value in zip(states, adam_update(master[...], moment[...], second[...], gradient[...])):
        ref[...] = value
    grad[...] = dot(move[...], rows, 0, 0).astype(BF16)


def last_body(new, new_other, order, *refs):
    held, outs, (out, sems) = refs[:4], refs[4:9], refs[9:]
    copies = []
    move = order[...]
    tile = out.shape[1] // OUT_COPIES
    half = new.shape[0]
    for i in range(OUT_COPIES):
        cols = pl.ds(i * tile, tile)
        chunk = dot(move[:half], new[:, cols], 0, 0) + dot(move[half:], new_other[:, cols], 0, 0)
        out[:, cols] = chunk.astype(BF16)
        copies.append(pltpu.make_async_copy(out.at[:, cols], outs[0].at[:, cols], sems.at[4 + i]))
        copies[-1].start()
        if i < len(held):
            copies.append(pltpu.make_async_copy(held[i], outs[1 + i], sems.at[i]))
            copies[-1].start()
    for copy in copies:
        copy.wait()


def local(hidden, cotangent, master, moment, second):
    reps, high = lax.axis_size("rep"), lax.axis_size("high")
    shards = high * LOW * CORES
    per, width = master.shape
    rows, part, tokens = shards * per, width // reps, hidden.shape[0]
    block = high * per
    factor = 1.0 / math.sqrt(tokens * reps * shards)
    far = [1 << i for i in range(high.bit_length() - 1)]
    halved, last = far[:-1], far[-1]
    near = sorted(((dx, low) for dx in range(reps) for low in range(LOW)),
                  key=lambda c: (c != (0, 0), -bool(c[0]) - bool(c[1]), c[::-1]))
    states = (master, moment, second)

    ins = [pltpu.with_memory_space_constraint(x, pltpu.HBM) for x in (hidden.T, cotangent)]
    keep, send, cot = call(
        functools.partial(partial_body, per, high),
        [((rows // 2, width), F32), ((rows // 2, width), BF16), (cotangent.shape, BF16)],
        "partial", ins,
        cost=2 * rows * width * tokens,
        in_specs=[pl.BlockSpec(memory_space=pltpu.HBM)] * 2,
        scratch_shapes=[pltpu.VMEM((rows, tokens), BF16), pltpu.SemaphoreType.DMA((COT_COPIES + 1,))],
    )

    recv = swap(send, 0, 0, 1)
    *pieces, state = call(
        functools.partial(middle_body, reps, near),
        [*((folded(block, part), BF16) if i else ((block, part), F32) for i in range(len(near))),
         (folded((reps + 3) * per, part), BF16)],
        "middle", [keep, recv, *states],
    )
    pieces = [pieces[0]] + [swap(p, dx, low) for p, (dx, low) in zip(pieces[1:], near[1:])]
    state_other = swap(state, 0, last * LOW)
    lines = block // 2
    body = functools.partial(plane_body, len(near))
    for bits in halved:
        keep, send = call(body, [((lines, part), F32), (folded(lines, part), BF16)], "halve", pieces)
        pieces, body, lines = [keep, swap(send, 0, bits * LOW)], halve_body, lines // 2
    (total,) = call(halve_body, [(folded(2 * per, part), BF16)], "whole", pieces)
    other = swap(total, 0, last * LOW)
    state, old = call(
        functools.partial(arrange_body, reps, per),
        [((3, 2 * per, part), F32), (folded(2 * per, width), BF16)],
        "arrange", [state, state_other, total],
    )
    grad, new = call(
        functools.partial(own_body, factor, per), [((per, part), BF16), (folded(2 * per, part), BF16)],
        "own", [total, other, state], cost=MAIN,
    )

    lines = 2 * per
    for bits in reversed(halved):
        body = functools.partial(join_body, lines)
        lines *= 2
        (new,) = call(body, [(folded(lines, part), BF16)], "copies", [new, swap(new, 0, bits * LOW)], cost=MAIN)
    grads = [grad] + [swap(grad, dx, 0) for dx in range(1, reps)]
    lines = 2 * per
    for chip in [bits * LOW for bits in reversed(halved)] + [1]:
        old_other = swap(old, 0, chip)
        shape = (2 * lines, width) if chip == 1 else folded(2 * lines, width)
        (old,) = call(functools.partial(join_body, lines), [(shape, BF16)], "join_old",
                      [old, old_other] + ([] if chip == 1 else [grad]))
        lines *= 2
    old_other = swap(old, 0, 0, 1)
    pieces = [swap(new, *c) if any(c) else new for c in near]
    (new,) = call(functools.partial(across_body, reps, near), [((rows // 2, width), BF16)],
                  "across", [old, *pieces])
    new_other = swap(new, 0, 0, 1)
    (grad,) = call(wide_body, [((per, width), F32)], "gradient", grads, cost=MAIN)
    outs = [((rows, tokens), BF16), *[((per, width), F32)] * 3]
    order, *held = call(functools.partial(product_body, per, high), [((rows, rows), BF16), *outs], "product",
                [old, old_other, cot, grad, *states], cost=2 * rows * width * tokens)
    outs = [((rows, width), BF16), *outs]
    updated, input_grad, *states = call(
        last_body, outs, "last", [new, new_other, order, *held],
        out_specs=(pl.BlockSpec(memory_space=pltpu.HBM),) * 5,
        scratch_shapes=[pltpu.VMEM(*outs[0]), pltpu.SemaphoreType.DMA((4 + OUT_COPIES,))],
    )
    return (input_grad.T, *states, updated)


def solution(mesh):
    reps, shards = mesh.shape["rep"], mesh.shape["shard"]
    split = Mesh(mesh.devices.reshape(reps, shards // LOW // CORES, LOW, CORES), (*CHIPS, "core"))
    by_row = P(("high", "low", "core"), None)
    by_token = P((*CHIPS, "core"), None)
    return jax.shard_map(
        local,
        mesh=split,
        in_specs=(by_token, by_token, by_row, by_row, by_row),
        out_specs=(by_token, by_row, by_row, by_row, P()),
        check_vma=False,
    )
```
